256 devices in a mesh: row: 32 (over x, y, core), col: 8 (over z).
Axes of the slice: x: 4, y: 4, z: 8, core: 2. Of those that a mesh axis runs over, the one named last changes fastest.
Arguments:
- kernel: float32 [3, 4096, 12, 1024], P(None, 'row', None, 'col'), as said below
Outputs:
- factored: float32 [3, 4096, 12, 1024], P(None, 'row', None, 'col')
Inputs may be any that keep to these rules, and one draw needn't show every extreme that they name: kernel read as an 12288 x 12288 matrix is symmetric positive definite.
All inputs are finite; a program needn't handle non-finite values.
Results may differ from the reference program's by a relative error of at most 0.0003.
Values sent between devices are 32-bit elements; how exact they have to be, the bound alone decides.
No kernel may reach another device: no remote copies, remote signals or barrier semaphores. Data moves between devices by JAX's collectives and lax.ppermute only.
A program may use at most 64 MiB of HBM per device.

```python
import jax
import jax.numpy as jnp
from jax import lax

M = 12288
NB = 128
PANEL = 512
RT = 3
CT = 12
N_ROW = 32
N_COL = 8


def draw_kernel(key, part):
    key = jax.random.fold_in(key, 7)
    feature_key, level_key = jax.random.split(key, 2)
    features = 3 * PANEL
    levels = jax.random.uniform(level_key, (M,), jnp.float32, 0.0, 1.0)
    samples = jax.random.normal(feature_key, (M, features), jnp.float32)
    inner_products = jnp.dot(samples, samples.T, precision=lax.Precision.HIGHEST) / features
    inner_products = (inner_products + inner_products.T) * 0.5
    matrix = inner_products + jnp.diag(0.2 + 0.3 * levels)
    return matrix.reshape(RT, N_ROW * NB, CT, N_COL * NB)


def setup_inputs(seed: int = 0) -> dict:
    seeds = jax.random.split(jax.random.key(seed), 2)
    return {
        "kernel": draw_kernel(jax.random.fold_in(seeds[1], 71), 0),
    }


HIGHEST = lax.Precision.HIGHEST

def reference(kernel):
    matrix = kernel.reshape(M, M)
    for number in range(2):
        column_start = number * PANEL
        after = column_start + PANEL
        diagonal_block = matrix[column_start:after, column_start:after]
        lower_factor = jnp.linalg.cholesky(diagonal_block)
        inverse_factor = lax.linalg.triangular_solve(lower_factor, jnp.eye(PANEL, dtype=jnp.float32), left_side=True, lower=True)
        solved_rows = jnp.dot(matrix[after:, column_start:after], inverse_factor.T, precision=HIGHEST)
        trailing = matrix[after:, after:] - jnp.dot(solved_rows, solved_rows.T, precision=HIGHEST)
        matrix = matrix.at[after:, after:].set(trailing)
        matrix = matrix.at[after:, column_start:after].set(solved_rows)
        matrix = matrix.at[column_start:after, column_start:after].set(lower_factor)
        matrix = matrix.at[:column_start, column_start:after].set(0.0)
        matrix = matrix.at[column_start:after, after:].set(0.0)
    return matrix.reshape(kernel.shape)
```

```python
import jax
import jax.numpy as jnp
from jax import lax
from jax.experimental import pallas as pl
from jax.experimental.pallas import tpu as pltpu
from jax.sharding import Mesh
from jax.sharding import PartitionSpec as P

TILE = 128
TILES = 8
WIDTH = TILE * TILES
HIGHEST = lax.Precision.HIGHEST
ROW = ("x", "y", "k")


def factor_tile(a_ref, v_ref):
    sub = lax.broadcasted_iota(jnp.int32, (8, TILE), 0)
    lane = lax.broadcasted_iota(jnp.int32, (8, TILE), 1)
    for t in range(TILE // 8):
        n = TILE // 8 - t
        rows = [slice(8 * (t + q), 8 * (t + q) + 8) for q in range(n)]
        a = [a_ref[s, :] for s in rows]
        if t == 0:
            v = [jnp.where(lane == sub + 8 * q, 1.0, 0.0) for q in range(n)]
        else:
            v = [v_ref[s, :] for s in rows]
        cols = [
            [jnp.broadcast_to(a[q][:, 8 * t + l : 8 * t + l + 1], (8, TILE)) for q in range(n)]
            for l in range(8)
        ]
        for j in range(8):
            pivot = jnp.broadcast_to(cols[j][0][j : j + 1, :], (8, TILE))
            inverse = 1.0 / pivot
            m = [cols[j][q] * inverse for q in range(n)]
            m[0] = jnp.where(sub > j, m[0], 0.0)
            for l in range(j + 1, 8):
                e = jnp.broadcast_to(cols[l][0][j : j + 1, :], (8, TILE))
                cols[l] = [cols[l][q] - m[q] * e for q in range(n)]
            ra = jnp.broadcast_to(a[0][j : j + 1, :], (8, TILE))
            a = [a[q] - m[q] * ra for q in range(n)]
            rv = jnp.broadcast_to(v[0][j : j + 1, :], (8, TILE))
            v = [v[q] - m[q] * rv for q in range(n)]
        pivots = cols[0][0]
        for j in range(1, 8):
            pivots = jnp.where(sub == j, cols[j][0], pivots)
        scale = lax.rsqrt(pivots)
        a[0] = jnp.where(lane >= sub + 8 * t, a[0] * scale, 0.0)
        v[0] = v[0] * scale
        for q in range(n):
            a_ref[rows[q], :] = a[q]
            v_ref[rows[q], :] = v[q]


def factor_kernel(x_ref, w_ref, u_ref, a_ref, v_ref):
    w_ref[...] = x_ref[...]

    def step(k, _):
        ks = pl.ds(pl.multiple_of(k * TILE, TILE), TILE)
        a_ref[...] = w_ref[ks, ks]
        factor_tile(a_ref, v_ref)
        u_ref[k] = a_ref[...]
        w_ref[ks, :] = jnp.dot(
            v_ref[...], w_ref[ks, :], precision=HIGHEST, preferred_element_type=jnp.float32
        )
        w_ref[ks, ks] = v_ref[...]

        def update(i, _):
            rows = pl.ds(pl.multiple_of(i * TILE, TILE), TILE)
            w_ref[rows, ks] = jnp.zeros((TILE, TILE), jnp.float32)
            w_ref[rows, :] -= lax.dot_general(
                w_ref[ks, rows],
                w_ref[ks, :],
                (((0,), (0,)), ((), ())),
                precision=HIGHEST,
                preferred_element_type=jnp.float32,
            )
            return 0

        lax.fori_loop(k + 1, TILES, update, 0)
        return 0

    lax.fori_loop(0, TILES, step, 0)


def factor(block):
    return pl.pallas_call(
        factor_kernel,
        out_shape=[
            jax.ShapeDtypeStruct((WIDTH, WIDTH), jnp.float32),
            jax.ShapeDtypeStruct((TILES, TILE, TILE), jnp.float32),
        ],
        scratch_shapes=[pltpu.VMEM((TILE, TILE), jnp.float32)] * 2,
        compiler_params=pltpu.CompilerParams(vmem_limit_bytes=40 << 20),
    )(block)


def spread_x(block):
    x = lax.axis_index("x")
    out = block
    for d in (1, 3, 2):
        out = jnp.where(x == d, lax.ppermute(block, "x", [(0, d)]), out)
    return out


def gather_z(block):
    n = lax.axis_size("z")
    me = lax.axis_index("z")
    parts = [block] + [
        lax.ppermute(block, "z", [((i + d) % n, i) for i in range(n)]) for d in range(1, n)
    ]
    rolled = jnp.concatenate(parts + parts, 0)
    return lax.dynamic_slice_in_dim(rolled, ((n - me) % n) * TILE, n * TILE, 0)


def body(kernel):
    row = lax.axis_index(ROW)
    col = lax.axis_index("z")
    strip = gather_z(spread_x(kernel[0, :, 0, :]).T)
    block = lax.all_gather(strip, ("y", "k"), axis=1, tiled=True)
    own = lax.all_gather(kernel[:, :, 0, :], "z", axis=2, tiled=True)
    head = spread_x(kernel[0, :, 1:, :].reshape(TILE, -1))
    right = lax.all_gather(head, ("y", "k"), axis=0, tiled=True)

    w, u = factor(block)
    tile = jnp.arange(WIDTH) // TILE
    linv = jnp.where(tile[:, None] >= tile[None, :], w, 0.0)
    solved = jnp.dot(own.reshape(-1, WIDTH), linv.T, precision=HIGHEST)
    twice = jnp.dot(solved, linv, precision=HIGHEST)
    product = jnp.dot(twice, right, precision=HIGHEST)
    product = product.reshape(3, TILE, 11, TILE)
    inside = row < TILES
    dead = (inside & (jnp.arange(3) == 0))[:, None, None, None]
    rest = jnp.where(dead, 0.0, kernel[:, :, 1:, :] - product)

    column = lax.dynamic_index_in_dim(solved.reshape(3, TILE, TILES, TILE), col, 2, False)
    low = lax.dynamic_slice(w, (col * TILE, row * TILE), (TILE, TILE))
    low = jnp.where(col == row, lax.dynamic_index_in_dim(u, col, 0, False), low).T
    low = jnp.where(col <= row, low, 0.0)
    column = jnp.where(dead[:, :, :, 0], low[None], column)
    return jnp.concatenate([column[:, :, None, :], rest], 2)


def solution(mesh):
    fine = Mesh(mesh.devices.reshape(4, 4, 2, 8), ("x", "y", "k", "z"))
    spec = P(None, ROW, None, "z")
    return jax.shard_map(body, mesh=fine, in_specs=(spec,), out_specs=spec, check_vma=False)
```

```python
import jax
import jax.numpy as jnp
from jax import lax
from jax.experimental import pallas as pl
from jax.experimental.pallas import tpu as pltpu
from jax.sharding import Mesh
from jax.sharding import PartitionSpec as P

TILE = 128
TILES = 8
WIDTH = TILE * TILES
GROUP = 16
ROW = ("x", "y", "k")
VMEM = pl.BlockSpec(memory_space=pltpu.VMEM)


def split(x):
    high = x.astype(jnp.bfloat16)
    rest = x - high.astype(jnp.float32)
    middle = rest.astype(jnp.bfloat16)
    return high, middle, (rest - middle.astype(jnp.float32)).astype(jnp.bfloat16)


def left_terms(parts, axis):
    h, m, l = parts
    return jnp.concatenate([h, h, m, h, l, m], axis)


def right_terms(parts, axis):
    h, m, l = parts
    return jnp.concatenate([h, m, h, l, h, m], axis)


def contract(a, b, da, db):
    return lax.dot_general(a, b, (((da,), (db,)), ((), ())), preferred_element_type=jnp.float32)


def spread_row(x, i):
    return jnp.broadcast_to(x[i : i + 1, :], (8, TILE))


def spread_col(x, i):
    return jnp.broadcast_to(x[:, i : i + 1], (8, TILE))


def factor_tile(a_ref, v_ref, hook):
    sub = lax.broadcasted_iota(jnp.int32, (8, TILE), 0)
    lane = lax.broadcasted_iota(jnp.int32, (8, TILE), 1)
    for t in range(TILE // GROUP):
        base = GROUP * t
        total = TILE // 8 - 2 * t
        n = min(4, total)
        rows = [slice(base + 8 * q, base + 8 * q + 8) for q in range(n)]
        a = [a_ref[s, :] for s in rows]
        if t == 0:
            v = [jnp.where(lane == sub + 8 * q, 1.0, 0.0) for q in range(n)]
        else:
            v = [v_ref[s, :] for s in rows]
        cols = [[spread_col(a[q], base + l) for q in range(n)] for l in range(GROUP)]

        def eliminate(j, inverse):
            q0, i = j // 8, j % 8
            m = [
                (cols[j][q] if q > q0 else jnp.where(sub > i, cols[j][q], 0.0)) * inverse
                for q in range(q0, n)
            ]
            for l in range(j + 1, GROUP):
                e = spread_row(cols[l][q0], i)
                for q in range(q0, n):
                    cols[l][q] = cols[l][q] - m[q - q0] * e
            ra, rv = spread_row(a[q0], i), spread_row(v[q0], i)
            for q in range(q0, n):
                a[q] = a[q] - m[q - q0] * ra
                v[q] = v[q] - m[q - q0] * rv

        for j in range(0, GROUP, 2):
            q0, i = j // 8, j % 8
            p = spread_row(cols[j][q0], i)
            g = spread_row(cols[j + 1][q0], i)
            d = spread_row(cols[j + 1][q0], i + 1)
            first = 1.0 / p
            second = p * (1.0 / (p * d - g * g))
            eliminate(j, first)
            eliminate(j + 1, second)
        for q in range(2):
            pivots = cols[8 * q][q]
            for i in range(1, 8):
                pivots = jnp.where(sub == i, cols[8 * q + i][q], pivots)
            scale = lax.rsqrt(pivots)
            a[q] = jnp.where(lane >= sub + base + 8 * q, a[q] * scale, 0.0)
            v[q] = v[q] * scale
        for q in range(n):
            a_ref[rows[q], :] = a[q]
            v_ref[rows[q], :] = v[q]
        if total > n:
            start = base + 8 * n
            done = jnp.concatenate(
                [jnp.concatenate(a[:2], 0), jnp.concatenate(v[:2], 0)], 1
            )
            parts = split(done)
            change = contract(
                left_terms(parts, 0)[:, :TILE], right_terms(parts, 0), 0, 0
            )[start:, :]
            if t == 0:
                shape = (TILE - start, TILE)
                diagonal = lax.broadcasted_iota(jnp.int32, shape, 0) + start
                diagonal = diagonal == lax.broadcasted_iota(jnp.int32, shape, 1)
                v_ref[start:, :] = jnp.where(diagonal, 1.0, 0.0) - change[:, TILE:]
            else:
                v_ref[start:, :] -= change[:, TILE:]
            a_ref[start:, :] -= change[:, :TILE]
        hook(t)


def factor_kernel(
    x_ref, w_ref, u_ref, a_ref, v_ref, vp_ref, vs_ref, h_ref, m_ref, l_ref, r_ref
):
    for i in range(TILES):
        for j in range(TILES):
            w_ref[i * TILE : (i + 1) * TILE, j * TILE : (j + 1) * TILE] = x_ref[i, j]
    w_ref[WIDTH:, :] = jnp.zeros((TILE, WIDTH), jnp.float32)
    a_ref[...] = x_ref[0, 0]
    vs_ref[...] = jnp.zeros_like(vs_ref)
    vp_ref[...] = jnp.zeros_like(vp_ref)

    def tile(i):
        return pl.ds(pl.multiple_of(i * TILE, TILE), TILE)

    def panel(row, column):
        w_ref[row, :] = contract(vs_ref[...], right_terms(split(w_ref[row, :]), 0), 1, 0)
        w_ref[row, column] = vp_ref[...]

    def steps(first, last, slots):
        def step(k, _):
            old = tile(jnp.where(k == 0, TILES, k - 1))
            column = tile(jnp.maximum(k - 1, 0))

            def hook(t):
                if t == 0:
                    panel(old, column)
                    parts = split(w_ref[old, :])
                    h_ref[...], m_ref[...], l_ref[...] = parts
                    r_ref[...] = right_terms(parts, 0)
                elif t <= slots:
                    i = k + t - 1
                    row = tile(jnp.minimum(i, TILES))
                    c = tile(jnp.minimum(i, TILES - 1))
                    w_ref[row, column] = jnp.zeros((TILE, TILE), jnp.float32)
                    left = left_terms((h_ref[:, c], m_ref[:, c], l_ref[:, c]), 0)
                    w_ref[row, :] -= contract(left, r_ref[...], 0, 0)

            factor_tile(a_ref, v_ref, hook)
            u_ref[k] = a_ref[...]
            vp_ref[...] = v_ref[...]
            vs_ref[...] = left_terms(split(v_ref[...]), 1)
            after = tile(jnp.minimum(k + 1, TILES - 1))
            ahead = contract(vs_ref[...], right_terms(split(w_ref[tile(k), after]), 0), 1, 0)
            parts = split(ahead)
            a_ref[...] = w_ref[after, after] - contract(
                left_terms(parts, 0), right_terms(parts, 0), 0, 0
            )
            return 0

        lax.fori_loop(first, last, step, 0)

    steps(0, 4, 7)
    steps(4, 8, 4)
    panel(tile(7), tile(7))


def factor(block):
    tile = pltpu.VMEM((TILE, TILE), jnp.float32)
    part = pltpu.VMEM((TILE, WIDTH), jnp.bfloat16)
    return pl.pallas_call(
        factor_kernel,
        out_shape=[
            jax.ShapeDtypeStruct((WIDTH + TILE, WIDTH), jnp.float32),
            jax.ShapeDtypeStruct((TILES, TILE, TILE), jnp.float32),
        ],
        in_specs=[VMEM],
        out_specs=[VMEM, VMEM],
        scratch_shapes=[tile, tile, tile, pltpu.VMEM((TILE, 6 * TILE), jnp.bfloat16)]
        + [part, part, part, pltpu.VMEM((6 * TILE, WIDTH), jnp.bfloat16)],
        compiler_params=pltpu.CompilerParams(vmem_limit_bytes=40 << 20),
        cost_estimate=pl.CostEstimate(flops=8 << 30, bytes_accessed=9 << 20, transcendentals=0),
        name="factor",
    )(block)


def solve_kernel(ids_ref, own_ref, w_ref, u_ref, t_ref, c_ref, s_ref, hl_ref):
    row, col = ids_ref[0], ids_ref[1]
    rows = own_ref.shape[1] * TILE
    own = split(
        jnp.concatenate([own_ref[z].reshape(rows, TILE) for z in range(TILES)], 1)
    )
    half = 2 * TILE
    lower = lax.broadcasted_iota(jnp.int32, (half, half), 0) // TILE
    lower = lower >= lax.broadcasted_iota(jnp.int32, (half, half), 1) // TILE
    for b in range(0, WIDTH, half):
        n = b + half
        block = w_ref[b:n, :n]
        edge = jnp.where(lower, block[:, b:n], 0.0)
        block = edge if b == 0 else jnp.concatenate([block[:, :b], edge], 1)
        parts = split(block)
        for i in range(3):
            hl_ref[i, b:n, :n] = parts[i]
        s_ref[:, b:n] = contract(
            left_terms([x[:, :n] for x in own], 1), right_terms(parts, 1), 1, 1
        )
    solved = split(s_ref[...])
    for b in range(0, WIDTH, half):
        right = right_terms([hl_ref[i, b:, b : b + half] for i in range(3)], 0)
        twice = contract(left_terms([x[:, b:] for x in solved], 1), right, 1, 0)
        high = twice.astype(jnp.bfloat16)
        t_ref[0, :, b : b + half] = high
        t_ref[1, :, b : b + half] = (twice - high.astype(jnp.float32)).astype(jnp.bfloat16)
    here = pl.ds(pl.multiple_of(col * TILE, TILE), TILE)
    c_ref[...] = s_ref[:, here].reshape(c_ref.shape)

    @pl.when(row < TILES)
    def _():
        there = pl.ds(pl.multiple_of(jnp.minimum(row, TILES - 1) * TILE, TILE), TILE)
        upper = jnp.where(col == row, u_ref[col], w_ref[here, there])
        c_ref[0] = jnp.where(col <= row, upper.T, 0.0)


def solve(ids, own, w, u):
    rows = own.shape[1] * TILE
    return pl.pallas_call(
        solve_kernel,
        out_shape=[
            jax.ShapeDtypeStruct((2, rows, WIDTH), jnp.bfloat16),
            jax.ShapeDtypeStruct((own.shape[1], TILE, TILE), jnp.float32),
        ],
        in_specs=[pl.BlockSpec(memory_space=pltpu.SMEM), VMEM, VMEM, VMEM],
        out_specs=[VMEM, VMEM],
        scratch_shapes=[
            pltpu.VMEM((rows, WIDTH), jnp.float32),
            pltpu.VMEM((3, WIDTH, WIDTH), jnp.bfloat16),
        ],
        compiler_params=pltpu.CompilerParams(vmem_limit_bytes=40 << 20),
        name="solve",
    )(ids, own, w, u)


def update_kernel(ids_ref, t_ref, c_ref, right_ref, k_ref, o_ref):
    step = pl.program_id(0)
    tiles, _, _ = c_ref.shape
    rows = tiles * TILE
    right = jnp.concatenate([right_ref[:, i].reshape(WIDTH, TILE) for i in range(2)], 1)
    high = right.astype(jnp.bfloat16)
    low = (right - high.astype(jnp.float32)).astype(jnp.bfloat16)
    left = jnp.concatenate([t_ref[0], t_ref[0], t_ref[1]], 1)
    product = contract(left, jnp.concatenate([high, low, high], 0), 1, 0)
    product = product.reshape(tiles, TILE, 2 * TILE)
    for i in range(2):
        o_ref[:, i] = k_ref[:, i] - product[:, :, i * TILE : (i + 1) * TILE]

    @pl.when(ids_ref[0] < TILES)
    def _():
        o_ref[0] = jnp.zeros(o_ref.shape[1:], jnp.float32)

    @pl.when(step == 0)
    def _():
        o_ref[:, 0] = c_ref[...]


def update(ids, t, c, right, kernel):
    tiles, columns = kernel.shape[:2]
    block = pl.BlockSpec((tiles, 2, TILE, TILE), lambda j: (0, j, 0, 0))
    return pl.pallas_call(
        update_kernel,
        grid=(columns // 2,),
        out_shape=jax.ShapeDtypeStruct(kernel.shape, jnp.float32),
        in_specs=[
            pl.BlockSpec(memory_space=pltpu.SMEM),
            VMEM,
            VMEM,
            pl.BlockSpec((TILES, 2, TILE, TILE), lambda j: (0, j, 0, 0)),
            block,
        ],
        out_specs=block,
        compiler_params=pltpu.CompilerParams(vmem_limit_bytes=40 << 20),
        name="update",
    )(ids, t, c, right, kernel)


def spread_x(block):
    x = lax.axis_index("x")
    out = block
    for d in (1, 3, 2):
        out = jnp.where(x == d, lax.ppermute(block, "x", [(0, d)]), out)
    return out


def gather_z(block):
    n = lax.axis_size("z")
    me = lax.axis_index("z")
    parts = [block] + [
        lax.ppermute(block, "z", [((i + d) % n, i) for i in range(n)]) for d in range(1, n)
    ]
    rolled = jnp.stack(parts + parts)
    return lax.dynamic_slice_in_dim(rolled, (n - me) % n, n, 0)


def body(kernel):
    kernel = kernel.transpose(0, 2, 1, 3)
    ids = jnp.stack([lax.axis_index(ROW), lax.axis_index("z")]).astype(jnp.int32)
    strip = gather_z(spread_x(kernel[0, 0]))
    block = lax.all_gather(strip, ("y", "k"))
    own = lax.all_gather(kernel[:, 0], "z")
    right = lax.all_gather(spread_x(kernel[0]), ("y", "k"))
    w, u = factor(block)
    t, c = solve(ids, own, w, u)
    out = update(ids, t, c, right, kernel)
    return out.transpose(0, 2, 1, 3)


def solution(mesh):
    fine = Mesh(mesh.devices.reshape(4, 4, 2, 8), ("x", "y", "k", "z"))
    spec = P(None, ROW, None, "z")
    return jax.shard_map(body, mesh=fine, in_specs=(spec,), out_specs=spec, check_vma=False)
```

```python
import jax
import jax.numpy as jnp
from jax import lax
from jax.experimental import pallas as pl
from jax.experimental.pallas import tpu as pltpu
from jax.sharding import Mesh
from jax.sharding import PartitionSpec as P

TILE = 128
TILES = 8
HALF = TILES // 2
WIDTH = TILE * TILES
PANEL = TILE * HALF
GROUP = 16
ROW = ("x", "y", "k")
VMEM = pl.BlockSpec(memory_space=pltpu.VMEM)
SMEM = pl.BlockSpec(memory_space=pltpu.SMEM)


def split(x):
    high = x.astype(jnp.bfloat16)
    rest = x - high.astype(jnp.float32)
    middle = rest.astype(jnp.bfloat16)
    return high, middle, (rest - middle.astype(jnp.float32)).astype(jnp.bfloat16)


def left_terms(parts, axis):
    h, m, l = parts
    return jnp.concatenate([h, h, m, h, l, m], axis)


def right_terms(parts, axis):
    h, m, l = parts
    return jnp.concatenate([h, m, h, l, h, m], axis)


def contract(a, b, da, db):
    return lax.dot_general(a, b, (((da,), (db,)), ((), ())), preferred_element_type=jnp.float32)


def tile(i):
    return pl.ds(pl.multiple_of(i * TILE, TILE), TILE)


def spread_row(x, i):
    return jnp.broadcast_to(x[i : i + 1, :], (8, TILE))


def spread_col(x, i):
    return jnp.broadcast_to(x[:, i : i + 1], (8, TILE))


def factor_tile(a_ref, v_ref, hook):
    sub = lax.broadcasted_iota(jnp.int32, (8, TILE), 0)
    lane = lax.broadcasted_iota(jnp.int32, (8, TILE), 1)
    for t in range(TILE // GROUP):
        base = GROUP * t
        total = TILE // 8 - 2 * t
        n = min(4, total)
        rows = [slice(base + 8 * q, base + 8 * q + 8) for q in range(n)]
        a = [a_ref[s, :] for s in rows]
        if t == 0:
            v = [jnp.where(lane == sub + 8 * q, 1.0, 0.0) for q in range(n)]
        else:
            v = [v_ref[s, :] for s in rows]
        cols = [[spread_col(a[q], base + l) for q in range(n)] for l in range(GROUP)]

        def eliminate(j, inverse):
            q0, i = j // 8, j % 8
            m = [
                (cols[j][q] if q > q0 else jnp.where(sub > i, cols[j][q], 0.0)) * inverse
                for q in range(q0, n)
            ]
            for l in range(j + 1, GROUP):
                e = spread_row(cols[l][q0], i)
                for q in range(q0, n):
                    cols[l][q] = cols[l][q] - m[q - q0] * e
            ra, rv = spread_row(a[q0], i), spread_row(v[q0], i)
            for q in range(q0, n):
                a[q] = a[q] - m[q - q0] * ra
                v[q] = v[q] - m[q - q0] * rv

        for j in range(0, GROUP, 2):
            q0, i = j // 8, j % 8
            p = spread_row(cols[j][q0], i)
            g = spread_row(cols[j + 1][q0], i)
            d = spread_row(cols[j + 1][q0], i + 1)
            first = 1.0 / p
            second = p * (1.0 / (p * d - g * g))
            eliminate(j, first)
            eliminate(j + 1, second)
        for q in range(2):
            pivots = cols[8 * q][q]
            for i in range(1, 8):
                pivots = jnp.where(sub == i, cols[8 * q + i][q], pivots)
            scale = lax.rsqrt(pivots)
            a[q] = jnp.where(lane >= sub + base + 8 * q, a[q] * scale, 0.0)
            v[q] = v[q] * scale
        for q in range(n):
            a_ref[rows[q], :] = a[q]
            v_ref[rows[q], :] = v[q]
        if total > n:
            start = base + 8 * n
            done = jnp.concatenate(
                [jnp.concatenate(a[:2], 0), jnp.concatenate(v[:2], 0)], 1
            )
            parts = split(done)
            change = contract(
                left_terms(parts, 0)[:, :TILE], right_terms(parts, 0), 0, 0
            )[start:, :]
            if t == 0:
                shape = (TILE - start, TILE)
                diagonal = lax.broadcasted_iota(jnp.int32, shape, 0) + start
                diagonal = diagonal == lax.broadcasted_iota(jnp.int32, shape, 1)
                v_ref[start:, :] = jnp.where(diagonal, 1.0, 0.0) - change[:, TILE:]
            else:
                v_ref[start:, :] -= change[:, TILE:]
            a_ref[start:, :] -= change[:, :TILE]
        hook(t)


def factor_panel(w_ref, a_ref, v_ref, vp_ref, vs_ref, h_ref, m_ref, l_ref, r_ref):
    w_ref[PANEL : PANEL + TILE, :] = jnp.zeros((TILE, PANEL), jnp.float32)
    a_ref[...] = w_ref[0:TILE, 0:TILE]
    vs_ref[...] = jnp.zeros_like(vs_ref)
    vp_ref[...] = jnp.zeros_like(vp_ref)

    def panel(row, column):
        w_ref[row, :] = contract(vs_ref[...], right_terms(split(w_ref[row, :]), 0), 1, 0)
        w_ref[row, column] = vp_ref[...]

    def step(k, _):
        old = tile(jnp.where(k == 0, HALF, k - 1))
        column = tile(jnp.maximum(k - 1, 0))

        def hook(t):
            if t == 0:
                panel(old, column)
                parts = split(w_ref[old, :])
                h_ref[...], m_ref[...], l_ref[...] = parts
                r_ref[...] = right_terms(parts, 0)
            elif t < HALF:
                i = k + t - 1
                row = tile(jnp.minimum(i, HALF))
                c = tile(jnp.minimum(i, HALF - 1))
                w_ref[row, column] = jnp.zeros((TILE, TILE), jnp.float32)
                left = left_terms((h_ref[:, c], m_ref[:, c], l_ref[:, c]), 0)
                w_ref[row, :] -= contract(left, r_ref[...], 0, 0)

        factor_tile(a_ref, v_ref, hook)
        w_ref[PANEL + TILE :, tile(k)] = a_ref[...]
        vp_ref[...] = v_ref[...]
        vs_ref[...] = left_terms(split(v_ref[...]), 1)
        after = tile(jnp.minimum(k + 1, HALF - 1))
        ahead = contract(vs_ref[...], right_terms(split(w_ref[tile(k), after]), 0), 1, 0)
        parts = split(ahead)
        a_ref[...] = w_ref[after, after] - contract(
            left_terms(parts, 0), right_terms(parts, 0), 0, 0
        )
        return 0

    lax.fori_loop(0, HALF, step, 0)
    panel(tile(HALF - 1), tile(HALF - 1))


def panel_scratch():
    square = pltpu.VMEM((TILE, TILE), jnp.float32)
    part = pltpu.VMEM((TILE, PANEL), jnp.bfloat16)
    return [square, square, square, pltpu.VMEM((TILE, 6 * TILE), jnp.bfloat16)] + [
        part,
        part,
        part,
        pltpu.VMEM((6 * TILE, PANEL), jnp.bfloat16),
    ]


FACTOR = (PANEL + 2 * TILE, PANEL)


def first_kernel(ids_ref, near_ref, far_ref, w_ref, *scratch):
    k = ids_ref[3]
    for ref, side in ((near_ref, k), (far_ref, 1 - k)):
        for y in range(2):
            for j in range(HALF):
                w_ref[tile(2 * y + side), j * TILE : (j + 1) * TILE] = ref[y, j]
    factor_panel(w_ref, *scratch)


def first(ids, near, far):
    return pl.pallas_call(
        first_kernel,
        out_shape=jax.ShapeDtypeStruct(FACTOR, jnp.float32),
        in_specs=[SMEM, VMEM, VMEM],
        out_specs=VMEM,
        scratch_shapes=panel_scratch(),
        compiler_params=pltpu.CompilerParams(vmem_limit_bytes=24 << 20),
        cost_estimate=pl.CostEstimate(flops=8 << 30, bytes_accessed=4 << 20, transcendentals=0),
        name="first",
    )(ids, near, far)


def factor_second(ids_ref, w0_ref, near_ref, far_ref, x_ref, w_ref, b_ref, *scratch):
    y, k = ids_ref[2], ids_ref[3]
    for ref, side in ((near_ref, k), (far_ref, 1 - k)):
        for d in range(4):
            row = tile(2 * lax.rem(y + 4 - d, 4) + side)
            for j in range(HALF):
                b_ref[row, j * TILE : (j + 1) * TILE] = ref[d, j]
    parts = split(b_ref[0:PANEL, :])
    for i in range(HALF):
        n = (i + 1) * TILE
        left = left_terms(split(w0_ref[n - TILE : n, :n]), 1)
        x_ref[n - TILE : n, :] = contract(left, right_terms([p[:n] for p in parts], 0), 1, 0)
    parts = split(x_ref[...])
    right = right_terms(parts, 0)
    for i in range(HALF):
        n = (i + 1) * TILE
        left = left_terms([p[:, n - TILE : n] for p in parts], 0)
        w_ref[n - TILE : n, :] = b_ref[PANEL + n - TILE : PANEL + n, :] - contract(
            left, right, 0, 0
        )
    factor_panel(w_ref, *scratch)


def apply_inverse(ids_ref, own_ref, w0_ref, x_ref, w1_ref, t_ref, c_ref, s_ref):
    row, col = ids_ref[0], ids_ref[1]
    rows = own_ref.shape[1] * TILE
    wide = 2 * TILE
    lower = lax.broadcasted_iota(jnp.int32, (wide, wide), 0) // TILE
    lower = lower >= lax.broadcasted_iota(jnp.int32, (wide, wide), 1) // TILE

    def inverse(w_ref):
        top = jnp.where(lower, w_ref[0:wide, 0:wide], 0.0)
        edge = jnp.where(lower, w_ref[wide:PANEL, wide:PANEL], 0.0)
        bottom = jnp.concatenate([w_ref[wide:PANEL, 0:wide], edge], 1)
        return split(top), split(bottom)

    def times_transpose(a, inv):
        a, (top, bottom) = split(a), inv
        return jnp.concatenate(
            [
                contract(left_terms([p[:, :wide] for p in a], 1), right_terms(top, 1), 1, 1),
                contract(left_terms(a, 1), right_terms(bottom, 1), 1, 1),
            ],
            1,
        )

    def times(a, inv):
        a, (top, bottom) = split(a), inv
        below = [p[:, wide:] for p in a]
        left = [jnp.concatenate([b[:, :wide]], 1) for b in bottom]
        both = [jnp.concatenate([t, l], 0) for t, l in zip(top, left)]
        right = [b[:, wide:] for b in bottom]
        return jnp.concatenate(
            [
                contract(left_terms(a, 1), right_terms(both, 0), 1, 0),
                contract(left_terms(below, 1), right_terms(right, 0), 1, 0),
            ],
            1,
        )

    def own(first):
        return jnp.concatenate(
            [own_ref[z].reshape(rows, TILE) for z in range(first, first + HALF)], 1
        )

    inv0, inv1 = inverse(w0_ref), inverse(w1_ref)
    x = split(x_ref[...])
    s0 = times_transpose(own(0), inv0)
    s_ref[:, :PANEL] = s0
    rest = own(HALF) - contract(left_terms(split(s0), 1), right_terms(x, 0), 1, 0)
    s1 = times_transpose(rest, inv1)
    s_ref[:, PANEL:] = s1
    t1 = times(s1, inv1)
    t0 = times(s0 - contract(left_terms(split(t1), 1), right_terms(x, 1), 1, 1), inv0)
    for start, t in ((0, t0), (PANEL, t1)):
        high = t.astype(jnp.bfloat16)
        t_ref[0, :, start : start + PANEL] = high
        t_ref[1, :, start : start + PANEL] = (t - high.astype(jnp.float32)).astype(jnp.bfloat16)
    c_ref[...] = s_ref[:, tile(col)].reshape(c_ref.shape)

    @pl.when(row < TILES)
    def _():
        c_ref[0] = jnp.zeros((TILE, TILE), jnp.float32)

    for first, w_ref in ((0, w0_ref), (HALF, w1_ref)):

        @pl.when((row >= first) & (row < first + HALF) & (col >= first) & (col <= row))
        def _(first=first, w_ref=w_ref):
            i, j = jnp.clip(col - first, 0, HALF - 1), jnp.clip(row - first, 0, HALF - 1)
            c_ref[0] = w_ref[tile(jnp.where(col == row, HALF + 1, i)), tile(j)].T

    @pl.when((row >= HALF) & (row < TILES) & (col < HALF))
    def _():
        i, j = jnp.clip(col, 0, HALF - 1), jnp.clip(row - HALF, 0, HALF - 1)
        c_ref[0] = x_ref[tile(i), tile(j)].T


def second_kernel(
    ids_ref, w0_ref, near_ref, far_ref, own_hbm, t_ref, c_ref,
    own_ref, arrived, x_ref, w1_ref, s_ref, b_ref, *scratch
):
    copy = pltpu.make_async_copy(own_hbm, own_ref, arrived)
    copy.start()
    factor_second(ids_ref, w0_ref, near_ref, far_ref, x_ref, w1_ref, b_ref, *scratch)
    copy.wait()
    apply_inverse(ids_ref, own_ref, w0_ref, x_ref, w1_ref, t_ref, c_ref, s_ref)


def second(ids, w0, near, far, own):
    rows = own.shape[1] * TILE
    return pl.pallas_call(
        second_kernel,
        out_shape=[
            jax.ShapeDtypeStruct((2, rows, WIDTH), jnp.bfloat16),
            jax.ShapeDtypeStruct((own.shape[1], TILE, TILE), jnp.float32),
        ],
        in_specs=[SMEM, VMEM, VMEM, VMEM, pl.BlockSpec(memory_space=pl.ANY)],
        out_specs=[VMEM, VMEM],
        scratch_shapes=[
            pltpu.VMEM(own.shape, jnp.float32),
            pltpu.SemaphoreType.DMA,
            pltpu.VMEM((PANEL, PANEL), jnp.float32),
            pltpu.VMEM(FACTOR, jnp.float32),
            pltpu.VMEM((rows, WIDTH), jnp.float32),
            pltpu.VMEM((WIDTH, PANEL), jnp.float32),
        ]
        + panel_scratch(),
        compiler_params=pltpu.CompilerParams(vmem_limit_bytes=40 << 20),
        cost_estimate=pl.CostEstimate(flops=16 << 30, bytes_accessed=8 << 20, transcendentals=0),
        name="second",
    )(ids, w0, near, far, own)


def update_kernel(ids_ref, t_ref, c_ref, right_ref, k_ref, o_ref):
    step = pl.program_id(0)
    tiles, _, _ = c_ref.shape
    rows = tiles * TILE
    quarters = [
        jnp.concatenate([right_ref[x, r, i] for r in range(TILES) for x in range(4)], 0)
        for i in range(2)
    ]
    right = jnp.concatenate(quarters, 1)
    high = right.astype(jnp.bfloat16)
    low = (right - high.astype(jnp.float32)).astype(jnp.bfloat16)
    left = jnp.concatenate([t_ref[0], t_ref[0], t_ref[1]], 1)
    product = contract(left, jnp.concatenate([high, low, high], 0), 1, 0)
    product = product.reshape(tiles, TILE, 2 * TILE)
    for i in range(2):
        o_ref[:, i] = k_ref[:, i] - product[:, :, i * TILE : (i + 1) * TILE]

    @pl.when(ids_ref[0] < TILES)
    def _():
        o_ref[0] = jnp.zeros(o_ref.shape[1:], jnp.float32)

    @pl.when(step == 0)
    def _():
        o_ref[:, 0] = c_ref[...]


def update(ids, t, c, right, kernel):
    tiles, columns = kernel.shape[:2]
    block = pl.BlockSpec((tiles, 2, TILE, TILE), lambda j: (0, j, 0, 0))
    return pl.pallas_call(
        update_kernel,
        grid=(columns // 2,),
        out_shape=jax.ShapeDtypeStruct(kernel.shape, jnp.float32),
        in_specs=[
            SMEM,
            VMEM,
            VMEM,
            pl.BlockSpec((4, TILES, 2, TILE // 4, TILE), lambda j: (0, 0, j, 0, 0)),
            block,
        ],
        out_specs=block,
        compiler_params=pltpu.CompilerParams(vmem_limit_bytes=44 << 20),
        name="update",
    )(ids, t, c, right, kernel)


def swap(x):
    return lax.ppermute(x, "k", [(0, 1), (1, 0)])


def send(x, axis, pairs):
    return lax.ppermute(x, axis, pairs)


def gather_first(strip):
    y = lax.axis_index("y")
    one = send(strip, "y", [(0, 1), (1, 0)])
    two = send(strip, "y", [(0, 3), (1, 2)])
    three = send(strip, "y", [(0, 2), (1, 3)])
    upper = jnp.where(y == 0, strip, jnp.where(y == 1, one, jnp.where(y == 2, three, two)))
    lower = jnp.where(y == 1, strip, jnp.where(y == 0, one, jnp.where(y == 2, two, three)))
    near = jnp.stack([upper, lower])
    return near, swap(near)


def gather_second(strip):
    n = lax.axis_size("y")
    return [strip] + [send(strip, "y", [(i, (i + d) % n) for i in range(n)]) for d in range(1, n)]


def body(kernel):
    kernel = kernel.transpose(0, 2, 1, 3)
    x = lax.axis_index("x")
    ids = jnp.stack([lax.axis_index(a) for a in (ROW, "z", "y", "k")]).astype(jnp.int32)
    own = lax.all_gather(kernel[:, 0], "z")

    corner = kernel[0, 0]
    for d in (1, 3, 2):
        corner = jnp.where(x == d, send(kernel[0, 0], "x", [(0, d)]), corner)
    corner, head = lax.optimization_barrier((corner, kernel[0]))
    spread = jnp.broadcast_to(corner, (TILES, TILE, TILE))
    strip = lax.all_to_all(spread, "z", 0, 0)
    quarters = head.reshape(-1, 4, TILE // 4, TILE)
    quarter = quarters[:, 0]
    for d in (1, 3, 2):
        quarter = jnp.where(x == d, send(quarters[:, d], "x", [(0, d)]), quarter)
    right = lax.all_gather(quarter, ROW)
    right = right.reshape(4, TILES, -1, TILE // 4, TILE)

    near, far = gather_first(strip[:HALF])
    near, far, rest = lax.optimization_barrier((near, far, strip[HALF:]))
    parts = gather_second(rest)
    w0 = first(ids, near, far)
    w0, parts = lax.optimization_barrier((w0, parts))
    more = jnp.stack(parts)
    t, c = second(ids, w0, more, swap(more), own)
    out = update(ids, t, c, right, kernel)
    return out.transpose(0, 2, 1, 3)


def solution(mesh):
    fine = Mesh(mesh.devices.reshape(4, 4, 2, 8), ("x", "y", "k", "z"))
    spec = P(None, ROW, None, "z")
    return jax.shard_map(body, mesh=fine, in_specs=(spec,), out_specs=spec, check_vma=False)
```

```python
import jax
import jax.numpy as jnp
from jax import lax
from jax.experimental import pallas as pl
from jax.experimental.pallas import tpu as pltpu
from jax.sharding import Mesh
from jax.sharding import PartitionSpec as P

TILE = 128
TILES = 8
HALF = TILES // 2
WIDTH = TILE * TILES
PANEL = TILE * HALF
GROUP = 16
GRANT = 24 << 20
ROW = ("x", "y", "k")
VMEM = pl.BlockSpec(memory_space=pltpu.VMEM)
SMEM = pl.BlockSpec(memory_space=pltpu.SMEM)


def split(x):
    high = x.astype(jnp.bfloat16)
    rest = x - high.astype(jnp.float32)
    middle = rest.astype(jnp.bfloat16)
    return high, middle, (rest - middle.astype(jnp.float32)).astype(jnp.bfloat16)


def left_terms(parts, axis):
    h, m, l = parts
    return jnp.concatenate([h, h, m, h, l, m], axis)


def right_terms(parts, axis):
    h, m, l = parts
    return jnp.concatenate([h, m, h, l, h, m], axis)


def contract(a, b, da, db):
    return lax.dot_general(a, b, (((da,), (db,)), ((), ())), preferred_element_type=jnp.float32)


def tile(i):
    return pl.ds(pl.multiple_of(i * TILE, TILE), TILE)


def spread_row(x, i):
    return jnp.broadcast_to(x[i : i + 1, :], (8, TILE))


def spread_col(x, i):
    return jnp.broadcast_to(x[:, i : i + 1], (8, TILE))


def factor_tile(a_ref, v_ref, hook):
    sub = lax.broadcasted_iota(jnp.int32, (8, TILE), 0)
    lane = lax.broadcasted_iota(jnp.int32, (8, TILE), 1)
    for t in range(TILE // GROUP):
        base = GROUP * t
        total = TILE // 8 - 2 * t
        n = min(4, total)
        rows = [slice(base + 8 * q, base + 8 * q + 8) for q in range(n)]
        a = [a_ref[s, :] for s in rows]
        if t == 0:
            v = [jnp.where(lane == sub + 8 * q, 1.0, 0.0) for q in range(n)]
        else:
            v = [v_ref[s, :] for s in rows]
        cols = [[spread_col(a[q], base + l) for q in range(n)] for l in range(GROUP)]

        def eliminate(j, inverse):
            q0, i = j // 8, j % 8
            m = [
                (cols[j][q] if q > q0 else jnp.where(sub > i, cols[j][q], 0.0)) * inverse
                for q in range(q0, n)
            ]
            for l in range(j + 1, GROUP):
                e = spread_row(cols[l][q0], i)
                for q in range(q0, n):
                    cols[l][q] = cols[l][q] - m[q - q0] * e
            ra, rv = spread_row(a[q0], i), spread_row(v[q0], i)
            for q in range(q0, n):
                a[q] = a[q] - m[q - q0] * ra
                v[q] = v[q] - m[q - q0] * rv

        for j in range(0, GROUP, 2):
            q0, i = j // 8, j % 8
            p = spread_row(cols[j][q0], i)
            g = spread_row(cols[j + 1][q0], i)
            d = spread_row(cols[j + 1][q0], i + 1)
            first = 1.0 / p
            second = p * (1.0 / (p * d - g * g))
            eliminate(j, first)
            eliminate(j + 1, second)
        for q in range(2):
            pivots = cols[8 * q][q]
            for i in range(1, 8):
                pivots = jnp.where(sub == i, cols[8 * q + i][q], pivots)
            scale = lax.rsqrt(pivots)
            a[q] = jnp.where(lane >= sub + base + 8 * q, a[q] * scale, 0.0)
            v[q] = v[q] * scale
        for q in range(n):
            a_ref[rows[q], :] = a[q]
            v_ref[rows[q], :] = v[q]
        if total > n:
            start = base + 8 * n
            done = jnp.concatenate(
                [jnp.concatenate(a[:2], 0), jnp.concatenate(v[:2], 0)], 1
            )
            parts = split(done)
            change = contract(
                left_terms(parts, 0)[:, :TILE], right_terms(parts, 0), 0, 0
            )[start:, :]
            if t == 0:
                shape = (TILE - start, TILE)
                diagonal = lax.broadcasted_iota(jnp.int32, shape, 0) + start
                diagonal = diagonal == lax.broadcasted_iota(jnp.int32, shape, 1)
                v_ref[start:, :] = jnp.where(diagonal, 1.0, 0.0) - change[:, TILE:]
            else:
                v_ref[start:, :] -= change[:, TILE:]
            a_ref[start:, :] -= change[:, :TILE]
        hook(t)


def factor_panel(w_ref, a_ref, v_ref, vp_ref, vs_ref, h_ref, m_ref, l_ref, r_ref):
    w_ref[PANEL : PANEL + TILE, :] = jnp.zeros((TILE, PANEL), jnp.float32)
    a_ref[...] = w_ref[0:TILE, 0:TILE]
    vs_ref[...] = jnp.zeros_like(vs_ref)
    vp_ref[...] = jnp.zeros_like(vp_ref)

    def panel(row, column):
        w_ref[row, :] = contract(vs_ref[...], right_terms(split(w_ref[row, :]), 0), 1, 0)
        w_ref[row, column] = vp_ref[...]

    def step(k, _):
        old = tile(jnp.where(k == 0, HALF, k - 1))
        column = tile(jnp.maximum(k - 1, 0))

        def hook(t):
            if t == 0:
                panel(old, column)
                parts = split(w_ref[old, :])
                h_ref[...], m_ref[...], l_ref[...] = parts
                r_ref[...] = right_terms(parts, 0)
            elif t < HALF:
                i = k + t - 1
                row = tile(jnp.minimum(i, HALF))
                c = tile(jnp.minimum(i, HALF - 1))
                w_ref[row, column] = jnp.zeros((TILE, TILE), jnp.float32)
                left = left_terms((h_ref[:, c], m_ref[:, c], l_ref[:, c]), 0)
                w_ref[row, :] -= contract(left, r_ref[...], 0, 0)

        factor_tile(a_ref, v_ref, hook)
        w_ref[PANEL + TILE :, tile(k)] = a_ref[...]
        vp_ref[...] = v_ref[...]
        vs_ref[...] = left_terms(split(v_ref[...]), 1)
        after = tile(jnp.minimum(k + 1, HALF - 1))
        ahead = contract(vs_ref[...], right_terms(split(w_ref[tile(k), after]), 0), 1, 0)
        parts = split(ahead)
        a_ref[...] = w_ref[after, after] - contract(
            left_terms(parts, 0), right_terms(parts, 0), 0, 0
        )
        return 0

    lax.fori_loop(0, HALF, step, 0)
    panel(tile(HALF - 1), tile(HALF - 1))


def panel_scratch():
    square = pltpu.VMEM((TILE, TILE), jnp.float32)
    part = pltpu.VMEM((TILE, PANEL), jnp.bfloat16)
    return [square, square, square, pltpu.VMEM((TILE, 6 * TILE), jnp.bfloat16)] + [
        part,
        part,
        part,
        pltpu.VMEM((6 * TILE, PANEL), jnp.bfloat16),
    ]


FACTOR = (PANEL + 2 * TILE, PANEL)


def first_kernel(ids_ref, near_ref, far_ref, w_ref, *scratch):
    k = ids_ref[3]
    for ref, side in ((near_ref, k), (far_ref, 1 - k)):
        for y in range(2):
            for j in range(HALF):
                w_ref[tile(2 * y + side), j * TILE : (j + 1) * TILE] = ref[y, j]
    factor_panel(w_ref, *scratch)


def first(ids, near, far):
    return pl.pallas_call(
        first_kernel,
        out_shape=jax.ShapeDtypeStruct(FACTOR, jnp.float32),
        in_specs=[SMEM, VMEM, VMEM],
        out_specs=VMEM,
        scratch_shapes=panel_scratch(),
        compiler_params=pltpu.CompilerParams(vmem_limit_bytes=GRANT),
        cost_estimate=pl.CostEstimate(flops=8 << 30, bytes_accessed=4 << 20, transcendentals=0),
        name="first",
    )(ids, near, far)


def factor_second(ids_ref, w0_ref, near_ref, far_ref, x_ref, w_ref, b_ref, *scratch):
    y, k = ids_ref[2], ids_ref[3]
    for ref, side in ((near_ref, k), (far_ref, 1 - k)):
        for d in range(4):
            row = tile(2 * lax.rem(y + 4 - d, 4) + side)
            for j in range(HALF):
                b_ref[row, j * TILE : (j + 1) * TILE] = ref[d, j]
    parts = split(b_ref[0:PANEL, :])
    for i in range(HALF):
        n = (i + 1) * TILE
        left = left_terms(split(w0_ref[n - TILE : n, :n]), 1)
        x_ref[n - TILE : n, :] = contract(left, right_terms([p[:n] for p in parts], 0), 1, 0)
    parts = split(x_ref[...])
    right = right_terms(parts, 0)
    for i in range(HALF):
        n = (i + 1) * TILE
        left = left_terms([p[:, n - TILE : n] for p in parts], 0)
        w_ref[n - TILE : n, :] = b_ref[PANEL + n - TILE : PANEL + n, :] - contract(
            left, right, 0, 0
        )
    factor_panel(w_ref, *scratch)


def apply_inverse(ids_ref, own_ref, w0_ref, x_ref, w1_ref, t_ref, c_ref, s_ref):
    row, col = ids_ref[0], ids_ref[1]
    rows = own_ref.shape[1] * TILE
    wide = 2 * TILE
    lower = lax.broadcasted_iota(jnp.int32, (wide, wide), 0) // TILE
    lower = lower >= lax.broadcasted_iota(jnp.int32, (wide, wide), 1) // TILE

    def inverse(w_ref):
        top = jnp.where(lower, w_ref[0:wide, 0:wide], 0.0)
        edge = jnp.where(lower, w_ref[wide:PANEL, wide:PANEL], 0.0)
        bottom = jnp.concatenate([w_ref[wide:PANEL, 0:wide], edge], 1)
        return split(top), split(bottom)

    def times_transpose(a, inv):
        a, (top, bottom) = split(a), inv
        return jnp.concatenate(
            [
                contract(left_terms([p[:, :wide] for p in a], 1), right_terms(top, 1), 1, 1),
                contract(left_terms(a, 1), right_terms(bottom, 1), 1, 1),
            ],
            1,
        )

    def times(a, inv):
        a, (top, bottom) = split(a), inv
        below = [p[:, wide:] for p in a]
        left = [jnp.concatenate([b[:, :wide]], 1) for b in bottom]
        both = [jnp.concatenate([t, l], 0) for t, l in zip(top, left)]
        right = [b[:, wide:] for b in bottom]
        return jnp.concatenate(
            [
                contract(left_terms(a, 1), right_terms(both, 0), 1, 0),
                contract(left_terms(below, 1), right_terms(right, 0), 1, 0),
            ],
            1,
        )

    def own(first):
        return jnp.concatenate(
            [own_ref[z].reshape(rows, TILE) for z in range(first, first + HALF)], 1
        )

    inv0, inv1 = inverse(w0_ref), inverse(w1_ref)
    x = split(x_ref[...])
    s0 = times_transpose(own(0), inv0)
    s_ref[:, :PANEL] = s0
    rest = own(HALF) - contract(left_terms(split(s0), 1), right_terms(x, 0), 1, 0)
    s1 = times_transpose(rest, inv1)
    s_ref[:, PANEL:] = s1
    t1 = times(s1, inv1)
    t0 = times(s0 - contract(left_terms(split(t1), 1), right_terms(x, 1), 1, 1), inv0)
    for start, t in ((0, t0), (PANEL, t1)):
        high = t.astype(jnp.bfloat16)
        t_ref[0, :, start : start + PANEL] = high
        t_ref[1, :, start : start + PANEL] = (t - high.astype(jnp.float32)).astype(jnp.bfloat16)
    c_ref[...] = s_ref[:, tile(col)].reshape(c_ref.shape)

    @pl.when(row < TILES)
    def _():
        c_ref[0] = jnp.zeros((TILE, TILE), jnp.float32)

    for first, w_ref in ((0, w0_ref), (HALF, w1_ref)):

        @pl.when((row >= first) & (row < first + HALF) & (col >= first) & (col <= row))
        def _(first=first, w_ref=w_ref):
            i, j = jnp.clip(col - first, 0, HALF - 1), jnp.clip(row - first, 0, HALF - 1)
            c_ref[0] = w_ref[tile(jnp.where(col == row, HALF + 1, i)), tile(j)].T

    @pl.when((row >= HALF) & (row < TILES) & (col < HALF))
    def _():
        i, j = jnp.clip(col, 0, HALF - 1), jnp.clip(row - HALF, 0, HALF - 1)
        c_ref[0] = x_ref[tile(i), tile(j)].T


def second_kernel(
    ids_ref, w0_ref, near_ref, far_ref, own_hbm, t_hbm, c_hbm,
    t_ref, c_ref, own_ref, sems, x_ref, w1_ref, s_ref, b_ref, *scratch
):
    copy = pltpu.make_async_copy(own_hbm, own_ref, sems.at[0])
    copy.start()
    factor_second(ids_ref, w0_ref, near_ref, far_ref, x_ref, w1_ref, b_ref, *scratch)
    copy.wait()
    apply_inverse(ids_ref, own_ref, w0_ref, x_ref, w1_ref, t_ref, c_ref, s_ref)
    out = [
        pltpu.make_async_copy(t_ref, t_hbm, sems.at[1]),
        pltpu.make_async_copy(c_ref, c_hbm, sems.at[2]),
    ]
    for copy in out:
        copy.start()
    for copy in out:
        copy.wait()


def second(ids, w0, near, far, own):
    rows = own.shape[1] * TILE
    return pl.pallas_call(
        second_kernel,
        out_shape=[
            jax.ShapeDtypeStruct((2, rows, WIDTH), jnp.bfloat16),
            jax.ShapeDtypeStruct((own.shape[1], TILE, TILE), jnp.float32),
        ],
        in_specs=[SMEM, VMEM, VMEM, VMEM, pl.BlockSpec(memory_space=pl.ANY)],
        out_specs=[pl.BlockSpec(memory_space=pltpu.HBM)] * 2,
        scratch_shapes=[
            pltpu.VMEM((2, rows, WIDTH), jnp.bfloat16),
            pltpu.VMEM((own.shape[1], TILE, TILE), jnp.float32),
            pltpu.VMEM(own.shape, jnp.float32),
            pltpu.SemaphoreType.DMA((3,)),
            pltpu.VMEM((PANEL, PANEL), jnp.float32),
            pltpu.VMEM(FACTOR, jnp.float32),
            pltpu.VMEM((rows, WIDTH), jnp.float32),
            pltpu.VMEM((WIDTH, PANEL), jnp.float32),
        ]
        + panel_scratch(),
        compiler_params=pltpu.CompilerParams(vmem_limit_bytes=GRANT),
        cost_estimate=pl.CostEstimate(flops=16 << 30, bytes_accessed=8 << 20, transcendentals=0),
        name="second",
    )(ids, w0, near, far, own)


def update_kernel(ids_ref, t_ref, c_ref, right_ref, k_ref, o_ref):
    step = pl.program_id(0)
    tiles, _, _ = c_ref.shape
    rows = tiles * TILE
    quarters = [
        jnp.concatenate(
            [
                right_ref[x, r, i]
                for r in range(TILES)
                for x in range(4)
            ],
            0,
        )
        for i in range(2)
    ]
    right = jnp.concatenate(quarters, 1)
    high = right.astype(jnp.bfloat16)
    low = (right - high.astype(jnp.float32)).astype(jnp.bfloat16)
    left = jnp.concatenate([t_ref[0], t_ref[0], t_ref[1]], 1)
    product = contract(left, jnp.concatenate([high, low, high], 0), 1, 0)
    product = product.reshape(tiles, TILE, 2 * TILE)
    for i in range(2):
        o_ref[:, i] = k_ref[:, i] - product[:, :, i * TILE : (i + 1) * TILE]

    @pl.when(ids_ref[0] < TILES)
    def _():
        o_ref[0] = jnp.zeros(o_ref.shape[1:], jnp.float32)

    @pl.when(step == 0)
    def _():
        o_ref[:, 0] = c_ref[...]


def update(ids, t, c, right, kernel):
    tiles, columns = kernel.shape[:2]
    block = pl.BlockSpec((tiles, 2, TILE, TILE), lambda j: (0, j, 0, 0))
    return pl.pallas_call(
        update_kernel,
        grid=(columns // 2,),
        out_shape=jax.ShapeDtypeStruct(kernel.shape, jnp.float32),
        in_specs=[
            SMEM,
            VMEM,
            VMEM,
            pl.BlockSpec((4, TILES, 2, TILE // 4, TILE), lambda j: (0, 0, j, 0, 0)),
            block,
        ],
        out_specs=block,
        compiler_params=pltpu.CompilerParams(vmem_limit_bytes=60 << 20),
        name="update",
    )(ids, t, c, right, kernel)


def swap(x):
    return lax.ppermute(x, "k", [(0, 1), (1, 0)])


def send(x, axis, pairs):
    return lax.ppermute(x, axis, pairs)


def gather_first(strip):
    y = lax.axis_index("y")
    one = send(strip, "y", [(0, 1), (1, 0)])
    two = send(strip, "y", [(0, 3), (1, 2)])
    three = send(strip, "y", [(0, 2), (1, 3)])
    upper = jnp.where(y == 0, strip, jnp.where(y == 1, one, jnp.where(y == 2, three, two)))
    lower = jnp.where(y == 1, strip, jnp.where(y == 0, one, jnp.where(y == 2, two, three)))
    near = jnp.stack([upper, lower])
    return near, swap(near)


def round_y(block):
    n = lax.axis_size("y")
    return [block] + [send(block, "y", [(i, (i + d) % n) for i in range(n)]) for d in range(1, n)]


def gather_z(block, later):
    n = lax.axis_size("z")
    k, z = lax.axis_index("k"), lax.axis_index("z")
    pair = jnp.stack([block, swap(block)])
    parts = []
    for d in (1, 2, 3):
        up = [(i, (i + d) % n) for i in range(n)]
        down = [(n + i, n + (i - d) % n) for i in range(n)]
        parts.append(send(pair, ("k", "z"), up + down))
    far = send(block, "z", [(i, (i + n // 2) % n) for i in range(n)])
    parts, later = lax.optimization_barrier((parts, later))
    mine = jnp.stack([p[0] for p in parts])
    other = swap(jnp.stack([p[1] for p in parts]))
    below = jnp.where(k == 0, mine, other)
    above = jnp.where(k == 0, other, mine)
    ring = jnp.concatenate([block[None], above, far[None], below[::-1]])
    return lax.dynamic_slice_in_dim(jnp.concatenate([ring, ring]), (n - z) % n, n, 0), later


def body(kernel):
    kernel = kernel.transpose(0, 2, 1, 3)
    x = lax.axis_index("x")
    ids = jnp.stack([lax.axis_index(a) for a in (ROW, "z", "y", "k")]).astype(jnp.int32)
    own = lax.all_gather(kernel[:, 0], "z")

    corner = kernel[0, 0]
    for d in (1, 3, 2):
        corner = jnp.where(x == d, send(kernel[0, 0], "x", [(0, d)]), corner)
    strip, head = gather_z(corner, kernel[0])
    quarters = head.reshape(-1, 4, TILE // 4, TILE)
    pieces = [send(quarters[:, d], "x", [(0, d)]) for d in (1, 3, 2)]
    strip, pieces = lax.optimization_barrier((strip, pieces))
    quarter = quarters[:, 0]
    for d, piece in zip((1, 3, 2), pieces):
        quarter = jnp.where(x == d, piece, quarter)
    right = lax.all_gather(quarter, ROW)
    right = right.reshape(4, TILES, -1, TILE // 4, TILE)

    near, far = gather_first(strip[:HALF])
    near, far, rest, own = lax.optimization_barrier((near, far, strip[HALF:], own))
    parts = round_y(rest)
    w0 = first(ids, near, far)
    w0, parts = lax.optimization_barrier((w0, parts))
    more = jnp.stack(parts)
    t, c = second(ids, w0, more, swap(more), own)
    out = update(ids, t, c, right, kernel)
    return out.transpose(0, 2, 1, 3)


def solution(mesh):
    fine = Mesh(mesh.devices.reshape(4, 4, 2, 8), ("x", "y", "k", "z"))
    spec = P(None, ROW, None, "z")
    return jax.shard_map(body, mesh=fine, in_specs=(spec,), out_specs=spec, check_vma=False)
```

```python
import jax
import jax.numpy as jnp
from jax import lax
from jax.experimental import pallas as pl
from jax.experimental.pallas import tpu as pltpu
from jax.sharding import Mesh
from jax.sharding import PartitionSpec as P

TILE = 128
TILES = 8
HALF = TILES // 2
WIDTH = TILE * TILES
PANEL = TILE * HALF
GROUP = 16
GRANT = 24 << 20
ROW = ("x", "y", "k")
VMEM = pl.BlockSpec(memory_space=pltpu.VMEM)
SMEM = pl.BlockSpec(memory_space=pltpu.SMEM)


def split(x):
    high = x.astype(jnp.bfloat16)
    rest = x - high.astype(jnp.float32)
    middle = rest.astype(jnp.bfloat16)
    return high, middle, (rest - middle.astype(jnp.float32)).astype(jnp.bfloat16)


def left_terms(parts, axis):
    h, m, l = parts
    return jnp.concatenate([h, h, m, h, l, m], axis)


def right_terms(parts, axis):
    h, m, l = parts
    return jnp.concatenate([h, m, h, l, h, m], axis)


def left_two(parts, axis):
    h, m = parts[:2]
    return jnp.concatenate([h, h, m], axis)


def right_two(parts, axis):
    h, m = parts[:2]
    return jnp.concatenate([h, m, h], axis)


def contract(a, b, da, db):
    return lax.dot_general(a, b, (((da,), (db,)), ((), ())), preferred_element_type=jnp.float32)


def tile(i):
    return pl.ds(pl.multiple_of(i * TILE, TILE), TILE)


def spread_row(x, i):
    return jnp.broadcast_to(x[i : i + 1, :], (8, TILE))


def spread_col(x, i):
    return jnp.broadcast_to(x[:, i : i + 1], (8, TILE))


def factor_tile(a_ref, v_ref, hook):
    sub = lax.broadcasted_iota(jnp.int32, (8, TILE), 0)
    lane = lax.broadcasted_iota(jnp.int32, (8, TILE), 1)
    for t in range(TILE // GROUP):
        base = GROUP * t
        total = TILE // 8 - 2 * t
        n = min(4, total)
        rows = [slice(base + 8 * q, base + 8 * q + 8) for q in range(n)]
        a = [a_ref[s, :] for s in rows]
        if t == 0:
            v = [jnp.where(lane == sub + 8 * q, 1.0, 0.0) for q in range(n)]
        else:
            v = [v_ref[s, :] for s in rows]
        cols = [[spread_col(a[q], base + l) for q in range(n)] for l in range(GROUP)]

        def eliminate(j, inverse):
            q0, i = j // 8, j % 8
            m = [
                (cols[j][q] if q > q0 else jnp.where(sub > i, cols[j][q], 0.0)) * inverse
                for q in range(q0, n)
            ]
            for l in range(j + 1, GROUP):
                e = spread_row(cols[l][q0], i)
                for q in range(q0, n):
                    cols[l][q] = cols[l][q] - m[q - q0] * e
            ra, rv = spread_row(a[q0], i), spread_row(v[q0], i)
            for q in range(q0, n):
                a[q] = a[q] - m[q - q0] * ra
                v[q] = v[q] - m[q - q0] * rv

        for j in range(0, GROUP, 2):
            q0, i = j // 8, j % 8
            p = spread_row(cols[j][q0], i)
            g = spread_row(cols[j + 1][q0], i)
            d = spread_row(cols[j + 1][q0], i + 1)
            first = 1.0 / p
            second = p * (1.0 / (p * d - g * g))
            eliminate(j, first)
            eliminate(j + 1, second)
        for q in range(2):
            pivots = cols[8 * q][q]
            for i in range(1, 8):
                pivots = jnp.where(sub == i, cols[8 * q + i][q], pivots)
            scale = lax.rsqrt(pivots)
            a[q] = jnp.where(lane >= sub + base + 8 * q, a[q] * scale, 0.0)
            v[q] = v[q] * scale
        for q in range(n):
            a_ref[rows[q], :] = a[q]
            v_ref[rows[q], :] = v[q]
        if total > n:
            start = base + 8 * n
            done = jnp.concatenate(
                [jnp.concatenate(a[:2], 0), jnp.concatenate(v[:2], 0)], 1
            )
            parts = split(done)
            change = contract(
                left_terms(parts, 0)[:, :TILE], right_terms(parts, 0), 0, 0
            )[start:, :]
            if t == 0:
                shape = (TILE - start, TILE)
                diagonal = lax.broadcasted_iota(jnp.int32, shape, 0) + start
                diagonal = diagonal == lax.broadcasted_iota(jnp.int32, shape, 1)
                v_ref[start:, :] = jnp.where(diagonal, 1.0, 0.0) - change[:, TILE:]
            else:
                v_ref[start:, :] -= change[:, TILE:]
            a_ref[start:, :] -= change[:, :TILE]
        hook(t)


def factor_panel(w_ref, a_ref, v_ref, vp_ref, vs_ref, h_ref, m_ref, l_ref, r_ref):
    w_ref[PANEL : PANEL + TILE, :] = jnp.zeros((TILE, PANEL), jnp.float32)
    a_ref[...] = w_ref[0:TILE, 0:TILE]
    vs_ref[...] = jnp.zeros_like(vs_ref)
    vp_ref[...] = jnp.zeros_like(vp_ref)

    def panel(row, column):
        w_ref[row, :] = contract(vs_ref[...], right_terms(split(w_ref[row, :]), 0), 1, 0)
        w_ref[row, column] = vp_ref[...]

    def step(k, _):
        old = tile(jnp.where(k == 0, HALF, k - 1))
        column = tile(jnp.maximum(k - 1, 0))

        def hook(t):
            if t == 0:
                panel(old, column)
                parts = split(w_ref[old, :])
                h_ref[...], m_ref[...], l_ref[...] = parts
                r_ref[...] = right_terms(parts, 0)
            elif t < HALF:
                i = k + t - 1
                row = tile(jnp.minimum(i, HALF))
                c = tile(jnp.minimum(i, HALF - 1))
                w_ref[row, column] = jnp.zeros((TILE, TILE), jnp.float32)
                left = left_terms((h_ref[:, c], m_ref[:, c], l_ref[:, c]), 0)
                w_ref[row, :] -= contract(left, r_ref[...], 0, 0)

        factor_tile(a_ref, v_ref, hook)
        w_ref[PANEL + TILE :, tile(k)] = a_ref[...]
        vp_ref[...] = v_ref[...]
        vs_ref[...] = left_terms(split(v_ref[...]), 1)
        after = tile(jnp.minimum(k + 1, HALF - 1))
        ahead = contract(vs_ref[...], right_terms(split(w_ref[tile(k), after]), 0), 1, 0)
        parts = split(ahead)
        a_ref[...] = w_ref[after, after] - contract(
            left_terms(parts, 0), right_terms(parts, 0), 0, 0
        )
        return 0

    lax.fori_loop(0, HALF, step, 0)
    panel(tile(HALF - 1), tile(HALF - 1))


def panel_scratch():
    square = pltpu.VMEM((TILE, TILE), jnp.float32)
    part = pltpu.VMEM((TILE, PANEL), jnp.bfloat16)
    return [square, square, square, pltpu.VMEM((TILE, 6 * TILE), jnp.bfloat16)] + [
        part,
        part,
        part,
        pltpu.VMEM((6 * TILE, PANEL), jnp.bfloat16),
    ]


FACTOR = (PANEL + 2 * TILE, PANEL)


def first_kernel(ids_ref, near_ref, far_ref, w_ref, *scratch):
    k = ids_ref[3]
    for ref, side in ((near_ref, k), (far_ref, 1 - k)):
        for y in range(2):
            for j in range(HALF):
                w_ref[tile(2 * y + side), j * TILE : (j + 1) * TILE] = ref[y, j]
    factor_panel(w_ref, *scratch)


def first(ids, near, far):
    return pl.pallas_call(
        first_kernel,
        out_shape=jax.ShapeDtypeStruct(FACTOR, jnp.float32),
        in_specs=[SMEM, VMEM, VMEM],
        out_specs=VMEM,
        scratch_shapes=panel_scratch(),
        compiler_params=pltpu.CompilerParams(vmem_limit_bytes=GRANT),
        cost_estimate=pl.CostEstimate(flops=8 << 30, bytes_accessed=4 << 20, transcendentals=0),
        name="first",
    )(ids, near, far)


def factor_second(ids_ref, w0_ref, near_ref, far_ref, x_ref, w_ref, b_ref, *scratch):
    y, k = ids_ref[2], ids_ref[3]
    for ref, side in ((near_ref, k), (far_ref, 1 - k)):
        for d in range(4):
            row = tile(2 * lax.rem(y + 4 - d, 4) + side)
            for j in range(HALF):
                b_ref[row, j * TILE : (j + 1) * TILE] = ref[d, j]
    parts = split(b_ref[0:PANEL, :])
    for i in range(HALF):
        n = (i + 1) * TILE
        left = left_terms(split(w0_ref[n - TILE : n, :n]), 1)
        x_ref[n - TILE : n, :] = contract(left, right_terms([p[:n] for p in parts], 0), 1, 0)
    parts = split(x_ref[...])
    right = right_terms(parts, 0)
    for i in range(HALF):
        n = (i + 1) * TILE
        left = left_terms([p[:, n - TILE : n] for p in parts], 0)
        w_ref[n - TILE : n, :] = b_ref[PANEL + n - TILE : PANEL + n, :] - contract(
            left, right, 0, 0
        )
    factor_panel(w_ref, *scratch)


def apply_inverse(ids_ref, own_ref, w0_ref, x_ref, w1_ref, t_ref, c_ref, s_ref):
    row, col = ids_ref[0], ids_ref[1]
    rows = own_ref.shape[1] * TILE
    wide = 2 * TILE
    lower = lax.broadcasted_iota(jnp.int32, (wide, wide), 0) // TILE
    lower = lower >= lax.broadcasted_iota(jnp.int32, (wide, wide), 1) // TILE

    def inverse(w_ref):
        top = jnp.where(lower, w_ref[0:wide, 0:wide], 0.0)
        edge = jnp.where(lower, w_ref[wide:PANEL, wide:PANEL], 0.0)
        bottom = jnp.concatenate([w_ref[wide:PANEL, 0:wide], edge], 1)
        return split(top), split(bottom)

    def times_transpose(a, inv):
        a, (top, bottom) = split(a), inv
        return jnp.concatenate(
            [
                contract(left_two([p[:, :wide] for p in a], 1), right_two(top, 1), 1, 1),
                contract(left_two(a, 1), right_two(bottom, 1), 1, 1),
            ],
            1,
        )

    def times(a, inv):
        a, (top, bottom) = split(a), inv
        below = [p[:, wide:] for p in a]
        left = [jnp.concatenate([b[:, :wide]], 1) for b in bottom]
        both = [jnp.concatenate([t, l], 0) for t, l in zip(top, left)]
        right = [b[:, wide:] for b in bottom]
        return jnp.concatenate(
            [
                contract(left_two(a, 1), right_two(both, 0), 1, 0),
                contract(left_two(below, 1), right_two(right, 0), 1, 0),
            ],
            1,
        )

    def own(first):
        return jnp.concatenate(
            [own_ref[z].reshape(rows, TILE) for z in range(first, first + HALF)], 1
        )

    inv0, inv1 = inverse(w0_ref), inverse(w1_ref)
    x = split(x_ref[...])
    s0 = times_transpose(own(0), inv0)
    s_ref[:, :PANEL] = s0
    rest = own(HALF) - contract(left_two(split(s0), 1), right_two(x, 0), 1, 0)
    s1 = times_transpose(rest, inv1)
    s_ref[:, PANEL:] = s1
    t1 = times(s1, inv1)
    t0 = times(s0 - contract(left_two(split(t1), 1), right_two(x, 1), 1, 1), inv0)
    for start, t in ((0, t0), (PANEL, t1)):
        high = t.astype(jnp.bfloat16)
        t_ref[0, :, start : start + PANEL] = high
        t_ref[1, :, start : start + PANEL] = (t - high.astype(jnp.float32)).astype(jnp.bfloat16)
    c_ref[...] = s_ref[:, tile(col)].reshape(c_ref.shape)

    @pl.when(row < TILES)
    def _():
        c_ref[0] = jnp.zeros((TILE, TILE), jnp.float32)

    for first, w_ref in ((0, w0_ref), (HALF, w1_ref)):

        @pl.when((row >= first) & (row < first + HALF) & (col >= first) & (col <= row))
        def _(first=first, w_ref=w_ref):
            i, j = jnp.clip(col - first, 0, HALF - 1), jnp.clip(row - first, 0, HALF - 1)
            c_ref[0] = w_ref[tile(jnp.where(col == row, HALF + 1, i)), tile(j)].T

    @pl.when((row >= HALF) & (row < TILES) & (col < HALF))
    def _():
        i, j = jnp.clip(col, 0, HALF - 1), jnp.clip(row - HALF, 0, HALF - 1)
        c_ref[0] = x_ref[tile(i), tile(j)].T


def second_kernel(
    ids_ref, w0_ref, near_ref, far_ref, own_hbm, t_hbm, c_hbm,
    t_ref, c_ref, own_ref, sems, x_ref, w1_ref, s_ref, b_ref, *scratch
):
    copy = pltpu.make_async_copy(own_hbm, own_ref, sems.at[0])
    copy.start()
    factor_second(ids_ref, w0_ref, near_ref, far_ref, x_ref, w1_ref, b_ref, *scratch)
    copy.wait()
    apply_inverse(ids_ref, own_ref, w0_ref, x_ref, w1_ref, t_ref, c_ref, s_ref)
    out = [
        pltpu.make_async_copy(t_ref, t_hbm, sems.at[1]),
        pltpu.make_async_copy(c_ref, c_hbm, sems.at[2]),
    ]
    for copy in out:
        copy.start()
    for copy in out:
        copy.wait()


def second(ids, w0, near, far, own):
    rows = own.shape[1] * TILE
    return pl.pallas_call(
        second_kernel,
        out_shape=[
            jax.ShapeDtypeStruct((2, rows, WIDTH), jnp.bfloat16),
            jax.ShapeDtypeStruct((own.shape[1], TILE, TILE), jnp.float32),
        ],
        in_specs=[SMEM, VMEM, VMEM, VMEM, pl.BlockSpec(memory_space=pl.ANY)],
        out_specs=[pl.BlockSpec(memory_space=pltpu.HBM)] * 2,
        scratch_shapes=[
            pltpu.VMEM((2, rows, WIDTH), jnp.bfloat16),
            pltpu.VMEM((own.shape[1], TILE, TILE), jnp.float32),
            pltpu.VMEM(own.shape, jnp.float32),
            pltpu.SemaphoreType.DMA((3,)),
            pltpu.VMEM((PANEL, PANEL), jnp.float32),
            pltpu.VMEM(FACTOR, jnp.float32),
            pltpu.VMEM((rows, WIDTH), jnp.float32),
            pltpu.VMEM((WIDTH, PANEL), jnp.float32),
        ]
        + panel_scratch(),
        compiler_params=pltpu.CompilerParams(vmem_limit_bytes=GRANT),
        cost_estimate=pl.CostEstimate(flops=16 << 30, bytes_accessed=8 << 20, transcendentals=0),
        name="second",
    )(ids, w0, near, far, own)


def update_kernel(ids_ref, t_ref, c_ref, right_ref, k_ref, o_ref):
    step = pl.program_id(0)
    tiles, _, _ = c_ref.shape
    rows = tiles * TILE
    quarters = [
        jnp.concatenate(
            [
                right_ref[x, r, i]
                for r in range(TILES)
                for x in range(4)
            ],
            0,
        )
        for i in range(2)
    ]
    right = jnp.concatenate(quarters, 1)
    high = right.astype(jnp.bfloat16)
    low = (right - high.astype(jnp.float32)).astype(jnp.bfloat16)
    left = jnp.concatenate([t_ref[0], t_ref[0], t_ref[1]], 1)
    product = contract(left, jnp.concatenate([high, low, high], 0), 1, 0)
    product = product.reshape(tiles, TILE, 2 * TILE)
    for i in range(2):
        o_ref[:, i] = k_ref[:, i] - product[:, :, i * TILE : (i + 1) * TILE]

    @pl.when(ids_ref[0] < TILES)
    def _():
        o_ref[0] = jnp.zeros(o_ref.shape[1:], jnp.float32)

    @pl.when(step == 0)
    def _():
        o_ref[:, 0] = c_ref[...]


def update(ids, t, c, right, kernel):
    tiles, columns = kernel.shape[:2]
    block = pl.BlockSpec((tiles, 2, TILE, TILE), lambda j: (0, j, 0, 0))
    return pl.pallas_call(
        update_kernel,
        grid=(columns // 2,),
        out_shape=jax.ShapeDtypeStruct(kernel.shape, jnp.float32),
        in_specs=[
            SMEM,
            VMEM,
            VMEM,
            pl.BlockSpec((4, TILES, 2, TILE // 4, TILE), lambda j: (0, 0, j, 0, 0)),
            block,
        ],
        out_specs=block,
        compiler_params=pltpu.CompilerParams(vmem_limit_bytes=60 << 20),
        name="update",
    )(ids, t, c, right, kernel)


def swap(x):
    return lax.ppermute(x, "k", [(0, 1), (1, 0)])


def send(x, axis, pairs):
    return lax.ppermute(x, axis, pairs)


def gather_first(strip):
    y = lax.axis_index("y")
    one = send(strip, "y", [(0, 1), (1, 0)])
    two = send(strip, "y", [(0, 3), (1, 2)])
    three = send(strip, "y", [(0, 2), (1, 3)])
    upper = jnp.where(y == 0, strip, jnp.where(y == 1, one, jnp.where(y == 2, three, two)))
    lower = jnp.where(y == 1, strip, jnp.where(y == 0, one, jnp.where(y == 2, two, three)))
    near = jnp.stack([upper, lower])
    return near, swap(near)


def round_y(block):
    n = lax.axis_size("y")
    return [block] + [send(block, "y", [(i, (i + d) % n) for i in range(n)]) for d in range(1, n)]


def gather_z(block):
    n = lax.axis_size("z")
    k, z = lax.axis_index("k"), lax.axis_index("z")
    pair = jnp.stack([block, swap(block)])
    parts = []
    for d in (1, 2, 3):
        up = [(i, (i + d) % n) for i in range(n)]
        down = [(n + i, n + (i - d) % n) for i in range(n)]
        parts.append(send(pair, ("k", "z"), up + down))
    far = send(block, "z", [(i, (i + n // 2) % n) for i in range(n)])
    parts, far = lax.optimization_barrier((parts, far))
    mine = jnp.stack([p[0] for p in parts])
    other = swap(jnp.stack([p[1] for p in parts]))
    below = jnp.where(k == 0, mine, other)
    above = jnp.where(k == 0, other, mine)
    ring = jnp.concatenate([block[None], above, far[None], below[::-1]])
    return lax.dynamic_slice_in_dim(jnp.concatenate([ring, ring]), (n - z) % n, n, 0)


def body(kernel):
    kernel = kernel.transpose(0, 2, 1, 3)
    x = lax.axis_index("x")
    ids = jnp.stack([lax.axis_index(a) for a in (ROW, "z", "y", "k")]).astype(jnp.int32)
    mine, kernel = lax.optimization_barrier((kernel[:, 0], kernel))
    own = lax.all_gather(mine, "z")

    quarters = kernel[0].reshape(-1, 4, TILE // 4, TILE)
    corner, quarter = quarters[0], quarters[:, 0]
    for d in (1, 3, 2):
        both = send(jnp.concatenate([quarters[0], quarters[:, d]]), "x", [(0, d)])
        corner = jnp.where(x == d, both[:4], corner)
        quarter = jnp.where(x == d, both[4:], quarter)
    corner = corner.reshape(TILE, TILE)
    right = lax.all_gather(quarter, ROW)
    right = right.reshape(4, TILES, -1, TILE // 4, TILE)

    strip = gather_z(corner)
    near, far = gather_first(strip[:HALF])
    near, far, rest, own = lax.optimization_barrier((near, far, strip[HALF:], own))
    parts = round_y(rest)
    w0 = first(ids, near, far)
    w0, parts = lax.optimization_barrier((w0, parts))
    more = jnp.stack(parts)
    t, c = second(ids, w0, more, swap(more), own)
    out = update(ids, t, c, right, kernel)
    return out.transpose(0, 2, 1, 3)


def solution(mesh):
    fine = Mesh(mesh.devices.reshape(4, 4, 2, 8), ("x", "y", "k", "z"))
    spec = P(None, ROW, None, "z")
    return jax.shard_map(body, mesh=fine, in_specs=(spec,), out_specs=spec, check_vma=False)
```

```python
import jax
import jax.numpy as jnp
from jax import lax
from jax.experimental import pallas as pl
from jax.experimental.pallas import tpu as pltpu
from jax.sharding import Mesh
from jax.sharding import PartitionSpec as P

TILE = 128
TILES = 8
HALF = TILES // 2
WIDTH = TILE * TILES
PANEL = TILE * HALF
GROUP = 16
GRANT = 24 << 20
ROW = ("x", "y", "k")
VMEM = pl.BlockSpec(memory_space=pltpu.VMEM)
SMEM = pl.BlockSpec(memory_space=pltpu.SMEM)


def split(x):
    high = x.astype(jnp.bfloat16)
    rest = x - high.astype(jnp.float32)
    middle = rest.astype(jnp.bfloat16)
    return high, middle, (rest - middle.astype(jnp.float32)).astype(jnp.bfloat16)


def left_terms(parts, axis):
    h, m, l = parts
    return jnp.concatenate([h, h, m, h, l, m], axis)


def right_terms(parts, axis):
    h, m, l = parts
    return jnp.concatenate([h, m, h, l, h, m], axis)


def left_two(parts, axis):
    h, m = parts[:2]
    return jnp.concatenate([h, h, m], axis)


def right_two(parts, axis):
    h, m = parts[:2]
    return jnp.concatenate([h, m, h], axis)


def contract(a, b, da, db):
    return lax.dot_general(a, b, (((da,), (db,)), ((), ())), preferred_element_type=jnp.float32)


def tile(i):
    return pl.ds(pl.multiple_of(i * TILE, TILE), TILE)


def quarter_rows(i, x, d):
    quarter = TILE // 4
    start = i * TILE + lax.rem(x + 4 - d, 4) * quarter
    return pl.ds(pl.multiple_of(start, quarter), quarter)


def spread_row(x, i):
    return jnp.broadcast_to(x[i : i + 1, :], (8, TILE))


def spread_col(x, i):
    return jnp.broadcast_to(x[:, i : i + 1], (8, TILE))


def factor_tile(a_ref, v_ref, hook):
    sub = lax.broadcasted_iota(jnp.int32, (8, TILE), 0)
    lane = lax.broadcasted_iota(jnp.int32, (8, TILE), 1)
    for t in range(TILE // GROUP):
        base = GROUP * t
        total = TILE // 8 - 2 * t
        n = min(4, total)
        rows = [slice(base + 8 * q, base + 8 * q + 8) for q in range(n)]
        a = [a_ref[s, :] for s in rows]
        if t == 0:
            v = [jnp.where(lane == sub + 8 * q, 1.0, 0.0) for q in range(n)]
        else:
            v = [v_ref[s, :] for s in rows]
        cols = [[spread_col(a[q], base + l) for q in range(n)] for l in range(GROUP)]

        def eliminate(j, inverse):
            q0, i = j // 8, j % 8
            m = [
                (cols[j][q] if q > q0 else jnp.where(sub > i, cols[j][q], 0.0)) * inverse
                for q in range(q0, n)
            ]
            for l in range(j + 1, GROUP):
                e = spread_row(cols[l][q0], i)
                for q in range(q0, n):
                    cols[l][q] = cols[l][q] - m[q - q0] * e
            ra, rv = spread_row(a[q0], i), spread_row(v[q0], i)
            for q in range(q0, n):
                a[q] = a[q] - m[q - q0] * ra
                v[q] = v[q] - m[q - q0] * rv

        for j in range(0, GROUP, 2):
            q0, i = j // 8, j % 8
            p = spread_row(cols[j][q0], i)
            g = spread_row(cols[j + 1][q0], i)
            d = spread_row(cols[j + 1][q0], i + 1)
            first = 1.0 / p
            second = p * (1.0 / (p * d - g * g))
            eliminate(j, first)
            eliminate(j + 1, second)
        for q in range(2):
            pivots = cols[8 * q][q]
            for i in range(1, 8):
                pivots = jnp.where(sub == i, cols[8 * q + i][q], pivots)
            scale = lax.rsqrt(pivots)
            a[q] = jnp.where(lane >= sub + base + 8 * q, a[q] * scale, 0.0)
            v[q] = v[q] * scale
        for q in range(n):
            a_ref[rows[q], :] = a[q]
            v_ref[rows[q], :] = v[q]
        if total > n:
            start = base + 8 * n
            done = jnp.concatenate(
                [jnp.concatenate(a[:2], 0), jnp.concatenate(v[:2], 0)], 1
            )
            parts = split(done)
            change = contract(
                left_terms(parts, 0)[:, :TILE], right_terms(parts, 0), 0, 0
            )[start:, :]
            if t == 0:
                shape = (TILE - start, TILE)
                diagonal = lax.broadcasted_iota(jnp.int32, shape, 0) + start
                diagonal = diagonal == lax.broadcasted_iota(jnp.int32, shape, 1)
                v_ref[start:, :] = jnp.where(diagonal, 1.0, 0.0) - change[:, TILE:]
            else:
                v_ref[start:, :] -= change[:, TILE:]
            a_ref[start:, :] -= change[:, :TILE]
        hook(t)


def factor_panel(w_ref, a_ref, v_ref, vp_ref, vs_ref, h_ref, m_ref, l_ref, r_ref):
    w_ref[PANEL : PANEL + TILE, :] = jnp.zeros((TILE, PANEL), jnp.float32)
    a_ref[...] = w_ref[0:TILE, 0:TILE]
    vs_ref[...] = jnp.zeros_like(vs_ref)
    vp_ref[...] = jnp.zeros_like(vp_ref)

    def panel(row, column):
        w_ref[row, :] = contract(vs_ref[...], right_terms(split(w_ref[row, :]), 0), 1, 0)
        w_ref[row, column] = vp_ref[...]

    def step(k, _):
        old = tile(jnp.where(k == 0, HALF, k - 1))
        column = tile(jnp.maximum(k - 1, 0))

        def hook(t):
            if t == 0:
                panel(old, column)
                parts = split(w_ref[old, :])
                h_ref[...], m_ref[...], l_ref[...] = parts
                r_ref[...] = right_terms(parts, 0)
            elif t < HALF:
                i = k + t - 1
                row = tile(jnp.minimum(i, HALF))
                c = tile(jnp.minimum(i, HALF - 1))
                w_ref[row, column] = jnp.zeros((TILE, TILE), jnp.float32)
                left = left_terms((h_ref[:, c], m_ref[:, c], l_ref[:, c]), 0)
                w_ref[row, :] -= contract(left, r_ref[...], 0, 0)

        factor_tile(a_ref, v_ref, hook)
        w_ref[PANEL + TILE :, tile(k)] = a_ref[...]
        vp_ref[...] = v_ref[...]
        vs_ref[...] = left_terms(split(v_ref[...]), 1)
        after = tile(jnp.minimum(k + 1, HALF - 1))
        ahead = contract(vs_ref[...], right_terms(split(w_ref[tile(k), after]), 0), 1, 0)
        parts = split(ahead)
        a_ref[...] = w_ref[after, after] - contract(
            left_terms(parts, 0), right_terms(parts, 0), 0, 0
        )
        return 0

    lax.fori_loop(0, HALF, step, 0)
    panel(tile(HALF - 1), tile(HALF - 1))


def panel_scratch():
    square = pltpu.VMEM((TILE, TILE), jnp.float32)
    part = pltpu.VMEM((TILE, PANEL), jnp.bfloat16)
    return [square, square, square, pltpu.VMEM((TILE, 6 * TILE), jnp.bfloat16)] + [
        part,
        part,
        part,
        pltpu.VMEM((6 * TILE, PANEL), jnp.bfloat16),
    ]


FACTOR = (PANEL + 2 * TILE, PANEL)


def first_kernel(ids_ref, near_ref, far_ref, w_ref, *scratch):
    k, x = ids_ref[3], ids_ref[4]
    for ref, side in ((near_ref, k), (far_ref, 1 - k)):
        for d in range(4):
            for y in range(2):
                rows = quarter_rows(2 * y + side, x, d)
                for j in range(HALF):
                    w_ref[rows, j * TILE : (j + 1) * TILE] = ref[d, y, j]
    factor_panel(w_ref, *scratch)


def first(ids, near, far):
    return pl.pallas_call(
        first_kernel,
        out_shape=jax.ShapeDtypeStruct(FACTOR, jnp.float32),
        in_specs=[SMEM, VMEM, VMEM],
        out_specs=VMEM,
        scratch_shapes=panel_scratch(),
        compiler_params=pltpu.CompilerParams(vmem_limit_bytes=GRANT),
        cost_estimate=pl.CostEstimate(flops=8 << 30, bytes_accessed=4 << 20, transcendentals=0),
        name="first",
    )(ids, near, far)


def factor_second(ids_ref, w0_ref, near_ref, far_ref, x_ref, w_ref, b_ref, *scratch):
    y, k, x = ids_ref[2], ids_ref[3], ids_ref[4]
    for ref, side in ((near_ref, k), (far_ref, 1 - k)):
        for d in range(4):
            for e in range(4):
                rows = quarter_rows(2 * lax.rem(y + 4 - e, 4) + side, x, d)
                for j in range(HALF):
                    b_ref[rows, j * TILE : (j + 1) * TILE] = ref[d, e, j]
    parts = split(b_ref[0:PANEL, :])
    for i in range(HALF):
        n = (i + 1) * TILE
        left = left_terms(split(w0_ref[n - TILE : n, :n]), 1)
        x_ref[n - TILE : n, :] = contract(left, right_terms([p[:n] for p in parts], 0), 1, 0)
    parts = split(x_ref[...])
    right = right_terms(parts, 0)
    for i in range(HALF):
        n = (i + 1) * TILE
        left = left_terms([p[:, n - TILE : n] for p in parts], 0)
        w_ref[n - TILE : n, :] = b_ref[PANEL + n - TILE : PANEL + n, :] - contract(
            left, right, 0, 0
        )
    factor_panel(w_ref, *scratch)


def apply_inverse(ids_ref, own_ref, w0_ref, x_ref, w1_ref, t_ref, c_ref, s_ref):
    row, col = ids_ref[0], ids_ref[1]
    rows = own_ref.shape[1] * TILE
    wide = 2 * TILE
    lower = lax.broadcasted_iota(jnp.int32, (wide, wide), 0) // TILE
    lower = lower >= lax.broadcasted_iota(jnp.int32, (wide, wide), 1) // TILE

    def inverse(w_ref):
        top = jnp.where(lower, w_ref[0:wide, 0:wide], 0.0)
        edge = jnp.where(lower, w_ref[wide:PANEL, wide:PANEL], 0.0)
        bottom = jnp.concatenate([w_ref[wide:PANEL, 0:wide], edge], 1)
        return split(top), split(bottom)

    def times_transpose(a, inv):
        a, (top, bottom) = split(a), inv
        return jnp.concatenate(
            [
                contract(left_two([p[:, :wide] for p in a], 1), right_two(top, 1), 1, 1),
                contract(left_two(a, 1), right_two(bottom, 1), 1, 1),
            ],
            1,
        )

    def times(a, inv):
        a, (top, bottom) = split(a), inv
        below = [p[:, wide:] for p in a]
        left = [jnp.concatenate([b[:, :wide]], 1) for b in bottom]
        both = [jnp.concatenate([t, l], 0) for t, l in zip(top, left)]
        right = [b[:, wide:] for b in bottom]
        return jnp.concatenate(
            [
                contract(left_two(a, 1), right_two(both, 0), 1, 0),
                contract(left_two(below, 1), right_two(right, 0), 1, 0),
            ],
            1,
        )

    def own(first):
        return jnp.concatenate(
            [own_ref[z].reshape(rows, TILE) for z in range(first, first + HALF)], 1
        )

    inv0, inv1 = inverse(w0_ref), inverse(w1_ref)
    x = split(x_ref[...])
    s0 = times_transpose(own(0), inv0)
    s_ref[:, :PANEL] = s0
    rest = own(HALF) - contract(left_two(split(s0), 1), right_two(x, 0), 1, 0)
    s1 = times_transpose(rest, inv1)
    s_ref[:, PANEL:] = s1
    t1 = times(s1, inv1)
    t0 = times(s0 - contract(left_two(split(t1), 1), right_two(x, 1), 1, 1), inv0)
    for start, t in ((0, t0), (PANEL, t1)):
        high = t.astype(jnp.bfloat16)
        t_ref[0, :, start : start + PANEL] = high
        t_ref[1, :, start : start + PANEL] = (t - high.astype(jnp.float32)).astype(jnp.bfloat16)
    c_ref[...] = s_ref[:, tile(col)].reshape(c_ref.shape)

    @pl.when(row < TILES)
    def _():
        c_ref[0] = jnp.zeros((TILE, TILE), jnp.float32)

    for first, w_ref in ((0, w0_ref), (HALF, w1_ref)):

        @pl.when((row >= first) & (row < first + HALF) & (col >= first) & (col <= row))
        def _(first=first, w_ref=w_ref):
            i, j = jnp.clip(col - first, 0, HALF - 1), jnp.clip(row - first, 0, HALF - 1)
            c_ref[0] = w_ref[tile(jnp.where(col == row, HALF + 1, i)), tile(j)].T

    @pl.when((row >= HALF) & (row < TILES) & (col < HALF))
    def _():
        i, j = jnp.clip(col, 0, HALF - 1), jnp.clip(row - HALF, 0, HALF - 1)
        c_ref[0] = x_ref[tile(i), tile(j)].T


def second_kernel(
    ids_ref, w0_ref, near_ref, far_ref, own_hbm, t_hbm, c_hbm,
    t_ref, c_ref, own_ref, sems, x_ref, w1_ref, s_ref, b_ref, *scratch
):
    copy = pltpu.make_async_copy(own_hbm, own_ref, sems.at[0])
    copy.start()
    factor_second(ids_ref, w0_ref, near_ref, far_ref, x_ref, w1_ref, b_ref, *scratch)
    copy.wait()
    apply_inverse(ids_ref, own_ref, w0_ref, x_ref, w1_ref, t_ref, c_ref, s_ref)
    out = [
        pltpu.make_async_copy(t_ref, t_hbm, sems.at[1]),
        pltpu.make_async_copy(c_ref, c_hbm, sems.at[2]),
    ]
    for copy in out:
        copy.start()
    for copy in out:
        copy.wait()


def second(ids, w0, near, far, own):
    rows = own.shape[1] * TILE
    return pl.pallas_call(
        second_kernel,
        out_shape=[
            jax.ShapeDtypeStruct((2, rows, WIDTH), jnp.bfloat16),
            jax.ShapeDtypeStruct((own.shape[1], TILE, TILE), jnp.float32),
        ],
        in_specs=[SMEM, VMEM, VMEM, VMEM, pl.BlockSpec(memory_space=pl.ANY)],
        out_specs=[pl.BlockSpec(memory_space=pltpu.HBM)] * 2,
        scratch_shapes=[
            pltpu.VMEM((2, rows, WIDTH), jnp.bfloat16),
            pltpu.VMEM((own.shape[1], TILE, TILE), jnp.float32),
            pltpu.VMEM(own.shape, jnp.float32),
            pltpu.SemaphoreType.DMA((3,)),
            pltpu.VMEM((PANEL, PANEL), jnp.float32),
            pltpu.VMEM(FACTOR, jnp.float32),
            pltpu.VMEM((rows, WIDTH), jnp.float32),
            pltpu.VMEM((WIDTH, PANEL), jnp.float32),
        ]
        + panel_scratch(),
        compiler_params=pltpu.CompilerParams(vmem_limit_bytes=GRANT),
        cost_estimate=pl.CostEstimate(flops=16 << 30, bytes_accessed=8 << 20, transcendentals=0),
        name="second",
    )(ids, w0, near, far, own)


def update_kernel(ids_ref, t_ref, c_ref, even_ref, odd_ref, k_ref, o_ref):
    step = pl.program_id(0)
    tiles, _, _ = c_ref.shape
    rows = tiles * TILE
    quarters = [
        jnp.concatenate(
            [
                ref[x, r, 0]
                for r in range(TILES)
                for x in range(4)
            ],
            0,
        )
        for ref in (even_ref, odd_ref)
    ]
    right = jnp.concatenate(quarters, 1)
    high = right.astype(jnp.bfloat16)
    low = (right - high.astype(jnp.float32)).astype(jnp.bfloat16)
    left = jnp.concatenate([t_ref[0], t_ref[0], t_ref[1]], 1)
    product = contract(left, jnp.concatenate([high, low, high], 0), 1, 0)
    product = product.reshape(tiles, TILE, 2 * TILE)
    for i in range(2):
        o_ref[:, i] = k_ref[:, i] - product[:, :, i * TILE : (i + 1) * TILE]

    @pl.when(ids_ref[0] < TILES)
    def _():
        o_ref[0] = jnp.zeros(o_ref.shape[1:], jnp.float32)

    @pl.when(step == 0)
    def _():
        o_ref[:, 0] = c_ref[...]


def update(ids, t, c, right, kernel):
    tiles, columns = kernel.shape[:2]
    block = pl.BlockSpec((tiles, 2, TILE, TILE), lambda j: (0, j, 0, 0))
    piece = (4, TILES, 1, TILE // 4, TILE)
    return pl.pallas_call(
        update_kernel,
        grid=(columns // 2,),
        out_shape=jax.ShapeDtypeStruct(kernel.shape, jnp.float32),
        in_specs=[
            SMEM,
            VMEM,
            VMEM,
            pl.BlockSpec(piece, lambda j: (0, 0, jnp.maximum(2 * j - 1, 0), 0, 0)),
            pl.BlockSpec(piece, lambda j: (0, 0, 2 * j, 0, 0)),
            block,
        ],
        out_specs=block,
        compiler_params=pltpu.CompilerParams(vmem_limit_bytes=60 << 20),
        name="update",
    )(ids, t, c, right, right, kernel)


def swap(x):
    return lax.ppermute(x, "k", [(0, 1), (1, 0)])


def send(x, axis, pairs):
    return lax.ppermute(x, axis, pairs)


def around(block, axis):
    n = lax.axis_size(axis)
    return [block] + [send(block, axis, [(i, (i + d) % n) for i in range(n)]) for d in range(1, n)]


def gather_z(block):
    n = lax.axis_size("z")
    k, z = lax.axis_index("k"), lax.axis_index("z")
    pair = jnp.stack([block, swap(block)])
    parts = []
    for d in (1, 2, 3):
        up = [(i, (i + d) % n) for i in range(n)]
        down = [(n + i, n + (i - d) % n) for i in range(n)]
        parts.append(send(pair, ("k", "z"), up + down))
    far = send(block, "z", [(i, (i + n // 2) % n) for i in range(n)])
    parts, far = lax.optimization_barrier((parts, far))
    mine = jnp.stack([p[0] for p in parts])
    other = swap(jnp.stack([p[1] for p in parts]))
    below = jnp.where(k == 0, mine, other)
    above = jnp.where(k == 0, other, mine)
    ring = jnp.concatenate([block[None], above, far[None], below[::-1]])
    return lax.dynamic_slice_in_dim(jnp.concatenate([ring, ring]), (n - z) % n, n, 0)


def body(kernel):
    kernel = kernel.transpose(0, 2, 1, 3)
    x = lax.axis_index("x")
    y = lax.axis_index("y")
    places = (ROW, "z", "y", "k", "x")
    ids = jnp.stack([lax.axis_index(a) for a in places]).astype(jnp.int32)
    mine, kernel = lax.optimization_barrier((kernel[:, 0], kernel))
    own = lax.all_gather(mine, "z")

    quarters = kernel[0].reshape(-1, 4, TILE // 4, TILE)
    quarter = quarters[:, 0]
    for d in (1, 3, 2):
        quarter = jnp.where(x == d, send(quarters[:, d], "x", [(0, d)]), quarter)
    right = lax.all_gather(quarter[1:], ROW)
    right = right.reshape(4, TILES, -1, TILE // 4, TILE)

    strips = jnp.stack(around(gather_z(quarter[0]), "y"))
    top = [lax.dynamic_index_in_dim(strips, (y + 4 - i) % 4, 0, False)[:HALF] for i in range(2)]
    near = jnp.stack(around(jnp.stack(top), "x"))
    far = swap(near)
    near, far, rest, own = lax.optimization_barrier((near, far, strips[:, HALF:], own))
    parts = around(rest, "x")
    w0 = first(ids, near, far)
    w0, parts = lax.optimization_barrier((w0, parts))
    more = jnp.stack(parts)
    t, c = second(ids, w0, more, swap(more), own)
    out = update(ids, t, c, right, kernel)
    return out.transpose(0, 2, 1, 3)


def solution(mesh):
    fine = Mesh(mesh.devices.reshape(4, 4, 2, 8), ("x", "y", "k", "z"))
    spec = P(None, ROW, None, "z")
    return jax.shard_map(body, mesh=fine, in_specs=(spec,), out_specs=spec, check_vma=False)
```

```python
import jax
import jax.numpy as jnp
from jax import lax
from jax.experimental import pallas as pl
from jax.experimental.pallas import tpu as pltpu
from jax.sharding import Mesh
from jax.sharding import PartitionSpec as P

TILE = 128
TILES = 8
HALF = TILES // 2
WIDTH = TILE * TILES
PANEL = TILE * HALF
GROUP = 16
GRANT = 24 << 20
ROW = ("x", "y", "k")
VMEM = pl.BlockSpec(memory_space=pltpu.VMEM)
SMEM = pl.BlockSpec(memory_space=pltpu.SMEM)


def split(x):
    high = x.astype(jnp.bfloat16)
    rest = x - high.astype(jnp.float32)
    middle = rest.astype(jnp.bfloat16)
    return high, middle, (rest - middle.astype(jnp.float32)).astype(jnp.bfloat16)


def left_terms(parts, axis):
    h, m, l = parts
    return jnp.concatenate([h, h, m, h, l, m], axis)


def right_terms(parts, axis):
    h, m, l = parts
    return jnp.concatenate([h, m, h, l, h, m], axis)


def left_two(parts, axis):
    h, m = parts[:2]
    return jnp.concatenate([h, h, m], axis)


def right_two(parts, axis):
    h, m = parts[:2]
    return jnp.concatenate([h, m, h], axis)


def contract(a, b, da, db):
    return lax.dot_general(a, b, (((da,), (db,)), ((), ())), preferred_element_type=jnp.float32)


def tile(i):
    return pl.ds(pl.multiple_of(i * TILE, TILE), TILE)


def quarter_rows(i, x, d):
    quarter = TILE // 4
    start = i * TILE + lax.rem(x + 4 - d, 4) * quarter
    return pl.ds(pl.multiple_of(start, quarter), quarter)


def spread_row(x, i):
    return jnp.broadcast_to(x[i : i + 1, :], (8, TILE))


def spread_col(x, i):
    return jnp.broadcast_to(x[:, i : i + 1], (8, TILE))


def factor_tile(a_ref, v_ref, hook):
    sub = lax.broadcasted_iota(jnp.int32, (8, TILE), 0)
    lane = lax.broadcasted_iota(jnp.int32, (8, TILE), 1)
    for t in range(TILE // GROUP):
        base = GROUP * t
        total = TILE // 8 - 2 * t
        n = min(4, total)
        rows = [slice(base + 8 * q, base + 8 * q + 8) for q in range(n)]
        a = [a_ref[s, :] for s in rows]
        if t == 0:
            v = [jnp.where(lane == sub + 8 * q, 1.0, 0.0) for q in range(n)]
        else:
            v = [v_ref[s, :] for s in rows]
        cols = [[spread_col(a[q], base + l) for q in range(n)] for l in range(GROUP)]

        def eliminate(j, inverse):
            q0, i = j // 8, j % 8
            m = [
                (cols[j][q] if q > q0 else jnp.where(sub > i, cols[j][q], 0.0)) * inverse
                for q in range(q0, n)
            ]
            for l in range(j + 1, GROUP):
                e = spread_row(cols[l][q0], i)
                for q in range(q0, n):
                    cols[l][q] = cols[l][q] - m[q - q0] * e
            ra, rv = spread_row(a[q0], i), spread_row(v[q0], i)
            for q in range(q0, n):
                a[q] = a[q] - m[q - q0] * ra
                v[q] = v[q] - m[q - q0] * rv

        for j in range(0, GROUP, 2):
            q0, i = j // 8, j % 8
            p = spread_row(cols[j][q0], i)
            g = spread_row(cols[j + 1][q0], i)
            d = spread_row(cols[j + 1][q0], i + 1)
            first = 1.0 / p
            second = p * (1.0 / (p * d - g * g))
            eliminate(j, first)
            eliminate(j + 1, second)
        for q in range(2):
            pivots = cols[8 * q][q]
            for i in range(1, 8):
                pivots = jnp.where(sub == i, cols[8 * q + i][q], pivots)
            scale = lax.rsqrt(pivots)
            a[q] = jnp.where(lane >= sub + base + 8 * q, a[q] * scale, 0.0)
            v[q] = v[q] * scale
        for q in range(n):
            a_ref[rows[q], :] = a[q]
            v_ref[rows[q], :] = v[q]
        if total > n:
            start = base + 8 * n
            done = jnp.concatenate(
                [jnp.concatenate(a[:2], 0), jnp.concatenate(v[:2], 0)], 1
            )
            parts = split(done)
            change = contract(
                left_terms(parts, 0)[:, :TILE], right_terms(parts, 0), 0, 0
            )[start:, :]
            if t == 0:
                shape = (TILE - start, TILE)
                diagonal = lax.broadcasted_iota(jnp.int32, shape, 0) + start
                diagonal = diagonal == lax.broadcasted_iota(jnp.int32, shape, 1)
                v_ref[start:, :] = jnp.where(diagonal, 1.0, 0.0) - change[:, TILE:]
            else:
                v_ref[start:, :] -= change[:, TILE:]
            a_ref[start:, :] -= change[:, :TILE]
        hook(t)


def factor_panel(w_ref, a_ref, v_ref, vp_ref, vs_ref, h_ref, m_ref, l_ref, r_ref):
    w_ref[PANEL : PANEL + TILE, :] = jnp.zeros((TILE, PANEL), jnp.float32)
    a_ref[...] = w_ref[0:TILE, 0:TILE]
    vs_ref[...] = jnp.zeros_like(vs_ref)
    vp_ref[...] = jnp.zeros_like(vp_ref)

    def panel(row, column):
        w_ref[row, :] = contract(vs_ref[...], right_terms(split(w_ref[row, :]), 0), 1, 0)
        w_ref[row, column] = vp_ref[...]

    def step(k, _):
        old = tile(jnp.where(k == 0, HALF, k - 1))
        column = tile(jnp.maximum(k - 1, 0))

        def hook(t):
            if t == 0:
                panel(old, column)
                parts = split(w_ref[old, :])
                h_ref[...], m_ref[...], l_ref[...] = parts
                r_ref[...] = right_terms(parts, 0)
            elif t < HALF:
                i = k + t - 1
                row = tile(jnp.minimum(i, HALF))
                c = tile(jnp.minimum(i, HALF - 1))
                w_ref[row, column] = jnp.zeros((TILE, TILE), jnp.float32)
                left = left_terms((h_ref[:, c], m_ref[:, c], l_ref[:, c]), 0)
                w_ref[row, :] -= contract(left, r_ref[...], 0, 0)

        factor_tile(a_ref, v_ref, hook)
        w_ref[PANEL + TILE :, tile(k)] = a_ref[...]
        vp_ref[...] = v_ref[...]
        vs_ref[...] = left_terms(split(v_ref[...]), 1)
        after = tile(jnp.minimum(k + 1, HALF - 1))
        ahead = contract(vs_ref[...], right_terms(split(w_ref[tile(k), after]), 0), 1, 0)
        parts = split(ahead)
        a_ref[...] = w_ref[after, after] - contract(
            left_terms(parts, 0), right_terms(parts, 0), 0, 0
        )
        return 0

    lax.fori_loop(0, HALF, step, 0)
    panel(tile(HALF - 1), tile(HALF - 1))


def panel_scratch():
    square = pltpu.VMEM((TILE, TILE), jnp.float32)
    part = pltpu.VMEM((TILE, PANEL), jnp.bfloat16)
    return [square, square, square, pltpu.VMEM((TILE, 6 * TILE), jnp.bfloat16)] + [
        part,
        part,
        part,
        pltpu.VMEM((6 * TILE, PANEL), jnp.bfloat16),
    ]


FACTOR = (PANEL + 2 * TILE, PANEL)


def first_kernel(ids_ref, near_ref, far_ref, w_ref, *scratch):
    k, x = ids_ref[3], ids_ref[4]
    for ref, side in ((near_ref, k), (far_ref, 1 - k)):
        for d in range(4):
            for y in range(2):
                rows = quarter_rows(2 * y + side, x, d)
                for j in range(HALF):
                    w_ref[rows, j * TILE : (j + 1) * TILE] = ref[d, y, j]
    factor_panel(w_ref, *scratch)


def first(ids, near, far):
    return pl.pallas_call(
        first_kernel,
        out_shape=jax.ShapeDtypeStruct(FACTOR, jnp.float32),
        in_specs=[SMEM, VMEM, VMEM],
        out_specs=VMEM,
        scratch_shapes=panel_scratch(),
        compiler_params=pltpu.CompilerParams(vmem_limit_bytes=GRANT),
        cost_estimate=pl.CostEstimate(flops=8 << 30, bytes_accessed=4 << 20, transcendentals=0),
        name="first",
    )(ids, near, far)


def factor_second(ids_ref, w0_ref, near_ref, far_ref, x_ref, w_ref, b_ref, *scratch):
    k, x = ids_ref[3], ids_ref[4]
    for ref, side in ((near_ref, k), (far_ref, 1 - k)):
        for d in range(4):
            for e in range(4):
                rows = quarter_rows(2 * e + side, x, d)
                for j in range(HALF):
                    b_ref[rows, j * TILE : (j + 1) * TILE] = ref[d, e, j]
    parts = split(b_ref[0:PANEL, :])
    for i in range(HALF):
        n = (i + 1) * TILE
        left = left_terms(split(w0_ref[n - TILE : n, :n]), 1)
        x_ref[n - TILE : n, :] = contract(left, right_terms([p[:n] for p in parts], 0), 1, 0)
    parts = split(x_ref[...])
    right = right_terms(parts, 0)
    for i in range(HALF):
        n = (i + 1) * TILE
        left = left_terms([p[:, n - TILE : n] for p in parts], 0)
        w_ref[n - TILE : n, :] = b_ref[PANEL + n - TILE : PANEL + n, :] - contract(
            left, right, 0, 0
        )
    factor_panel(w_ref, *scratch)


def apply_inverse(ids_ref, own_ref, w0_ref, x_ref, w1_ref, t_ref, c_ref, s_ref):
    row, col = ids_ref[0], ids_ref[1]
    rows = own_ref.shape[1] * TILE
    wide = 2 * TILE
    lower = lax.broadcasted_iota(jnp.int32, (wide, wide), 0) // TILE
    lower = lower >= lax.broadcasted_iota(jnp.int32, (wide, wide), 1) // TILE

    def inverse(w_ref):
        top = jnp.where(lower, w_ref[0:wide, 0:wide], 0.0)
        edge = jnp.where(lower, w_ref[wide:PANEL, wide:PANEL], 0.0)
        bottom = jnp.concatenate([w_ref[wide:PANEL, 0:wide], edge], 1)
        return split(top), split(bottom)

    def times_transpose(a, inv):
        a, (top, bottom) = split(a), inv
        return jnp.concatenate(
            [
                contract(left_two([p[:, :wide] for p in a], 1), right_two(top, 1), 1, 1),
                contract(left_two(a, 1), right_two(bottom, 1), 1, 1),
            ],
            1,
        )

    def times(a, inv):
        a, (top, bottom) = split(a), inv
        below = [p[:, wide:] for p in a]
        left = [jnp.concatenate([b[:, :wide]], 1) for b in bottom]
        both = [jnp.concatenate([t, l], 0) for t, l in zip(top, left)]
        right = [b[:, wide:] for b in bottom]
        return jnp.concatenate(
            [
                contract(left_two(a, 1), right_two(both, 0), 1, 0),
                contract(left_two(below, 1), right_two(right, 0), 1, 0),
            ],
            1,
        )

    def own(first):
        return jnp.concatenate(
            [own_ref[z].reshape(rows, TILE) for z in range(first, first + HALF)], 1
        )

    inv0, inv1 = inverse(w0_ref), inverse(w1_ref)
    x = split(x_ref[...])
    s0 = times_transpose(own(0), inv0)
    s_ref[:, :PANEL] = s0
    rest = own(HALF) - contract(left_two(split(s0), 1), right_two(x, 0), 1, 0)
    s1 = times_transpose(rest, inv1)
    s_ref[:, PANEL:] = s1
    t1 = times(s1, inv1)
    t0 = times(s0 - contract(left_two(split(t1), 1), right_two(x, 1), 1, 1), inv0)
    for start, t in ((0, t0), (PANEL, t1)):
        high = t.astype(jnp.bfloat16)
        t_ref[0, :, start : start + PANEL] = high
        t_ref[1, :, start : start + PANEL] = (t - high.astype(jnp.float32)).astype(jnp.bfloat16)
    c_ref[...] = s_ref[:, tile(col)].reshape(c_ref.shape)

    @pl.when(row < TILES)
    def _():
        c_ref[0] = jnp.zeros((TILE, TILE), jnp.float32)

    for first, w_ref in ((0, w0_ref), (HALF, w1_ref)):

        @pl.when((row >= first) & (row < first + HALF) & (col >= first) & (col <= row))
        def _(first=first, w_ref=w_ref):
            i, j = jnp.clip(col - first, 0, HALF - 1), jnp.clip(row - first, 0, HALF - 1)
            c_ref[0] = w_ref[tile(jnp.where(col == row, HALF + 1, i)), tile(j)].T

    @pl.when((row >= HALF) & (row < TILES) & (col < HALF))
    def _():
        i, j = jnp.clip(col, 0, HALF - 1), jnp.clip(row - HALF, 0, HALF - 1)
        c_ref[0] = x_ref[tile(i), tile(j)].T


def second_kernel(
    ids_ref, w0_ref, near_ref, far_ref, own_hbm, t_hbm, c_hbm,
    t_ref, c_ref, own_ref, sems, x_ref, w1_ref, s_ref, b_ref, *scratch
):
    copy = pltpu.make_async_copy(own_hbm, own_ref, sems.at[0])
    copy.start()
    factor_second(ids_ref, w0_ref, near_ref, far_ref, x_ref, w1_ref, b_ref, *scratch)
    copy.wait()
    apply_inverse(ids_ref, own_ref, w0_ref, x_ref, w1_ref, t_ref, c_ref, s_ref)
    out = [
        pltpu.make_async_copy(t_ref, t_hbm, sems.at[1]),
        pltpu.make_async_copy(c_ref, c_hbm, sems.at[2]),
    ]
    for copy in out:
        copy.start()
    for copy in out:
        copy.wait()


def second(ids, w0, near, far, own):
    rows = own.shape[1] * TILE
    return pl.pallas_call(
        second_kernel,
        out_shape=[
            jax.ShapeDtypeStruct((2, rows, WIDTH), jnp.bfloat16),
            jax.ShapeDtypeStruct((own.shape[1], TILE, TILE), jnp.float32),
        ],
        in_specs=[SMEM, VMEM, VMEM, VMEM, pl.BlockSpec(memory_space=pl.ANY)],
        out_specs=[pl.BlockSpec(memory_space=pltpu.HBM)] * 2,
        scratch_shapes=[
            pltpu.VMEM((2, rows, WIDTH), jnp.bfloat16),
            pltpu.VMEM((own.shape[1], TILE, TILE), jnp.float32),
            pltpu.VMEM(own.shape, jnp.float32),
            pltpu.SemaphoreType.DMA((3,)),
            pltpu.VMEM((PANEL, PANEL), jnp.float32),
            pltpu.VMEM(FACTOR, jnp.float32),
            pltpu.VMEM((rows, WIDTH), jnp.float32),
            pltpu.VMEM((WIDTH, PANEL), jnp.float32),
        ]
        + panel_scratch(),
        compiler_params=pltpu.CompilerParams(vmem_limit_bytes=GRANT),
        cost_estimate=pl.CostEstimate(flops=16 << 30, bytes_accessed=8 << 20, transcendentals=0),
        name="second",
    )(ids, w0, near, far, own)


def update_kernel(ids_ref, t_ref, c_ref, even_ref, odd_ref, k_ref, o_ref):
    step = pl.program_id(0)
    tiles, _, _ = c_ref.shape
    rows = tiles * TILE
    right = jnp.concatenate([ref[...].reshape(WIDTH, TILE) for ref in (even_ref, odd_ref)], 1)
    high = right.astype(jnp.bfloat16)
    low = (right - high.astype(jnp.float32)).astype(jnp.bfloat16)
    left = jnp.concatenate([t_ref[0], t_ref[0], t_ref[1]], 1)
    product = contract(left, jnp.concatenate([high, low, high], 0), 1, 0)
    product = product.reshape(tiles, TILE, 2 * TILE)
    for i in range(2):
        o_ref[:, i] = k_ref[:, i] - product[:, :, i * TILE : (i + 1) * TILE]

    @pl.when(ids_ref[0] < TILES)
    def _():
        o_ref[0] = jnp.zeros(o_ref.shape[1:], jnp.float32)

    @pl.when(step == 0)
    def _():
        o_ref[:, 0] = c_ref[...]


def update(ids, t, c, right, kernel):
    tiles, columns = kernel.shape[:2]
    block = pl.BlockSpec((tiles, 2, TILE, TILE), lambda j: (0, j, 0, 0))
    piece = (TILES, 1, TILE, TILE)
    return pl.pallas_call(
        update_kernel,
        grid=(columns // 2,),
        out_shape=jax.ShapeDtypeStruct(kernel.shape, jnp.float32),
        in_specs=[
            SMEM,
            VMEM,
            VMEM,
            pl.BlockSpec(piece, lambda j: (0, jnp.maximum(2 * j - 1, 0), 0, 0)),
            pl.BlockSpec(piece, lambda j: (0, 2 * j, 0, 0)),
            block,
        ],
        out_specs=block,
        compiler_params=pltpu.CompilerParams(vmem_limit_bytes=60 << 20),
        name="update",
    )(ids, t, c, right, right, kernel)


def swap(x):
    return lax.ppermute(x, "k", [(0, 1), (1, 0)])


def send(x, axis, pairs):
    return lax.ppermute(x, axis, pairs)


def around(block, axis):
    n = lax.axis_size(axis)
    return [block] + [send(block, axis, [(i, (i + d) % n) for i in range(n)]) for d in range(1, n)]


def body(kernel):
    kernel = kernel.transpose(0, 2, 1, 3)
    x = lax.axis_index("x")
    places = (ROW, "z", "y", "k", "x")
    ids = jnp.stack([lax.axis_index(a) for a in places]).astype(jnp.int32)
    mine, kernel = lax.optimization_barrier((kernel[:, 0], kernel))
    own = lax.all_gather(mine, "z")

    quarters = kernel[0, 0].reshape(4, TILE // 4, TILE)
    quarter = quarters[0]
    for d in (1, 3, 2):
        quarter = jnp.where(x == d, send(quarters[d], "x", [(0, d)]), quarter)
    quarter, head = lax.optimization_barrier((quarter, kernel[0, 1:]))
    heads = [send(head, "x", [(0, d)]) for d in (1, 3, 2)]

    strips = jnp.broadcast_to(quarter, (4 * TILES, TILE // 4, TILE))
    strips = lax.all_to_all(strips, ("y", "z"), 0, 0).reshape(4, TILES, TILE // 4, TILE)
    near = around(strips[:2, :HALF], "x")
    near, heads = lax.optimization_barrier((near, heads))
    for d, block in zip((1, 3, 2), heads):
        head = jnp.where(x == d, block, head)
    right = lax.all_gather(head, ("y", "k"))
    near = jnp.stack(near)
    far = swap(near)
    near, far, rest, own = lax.optimization_barrier((near, far, strips[:, HALF:], own))
    parts = around(rest, "x")
    w0 = first(ids, near, far)
    w0, parts = lax.optimization_barrier((w0, parts))
    more = jnp.stack(parts)
    t, c = second(ids, w0, more, swap(more), own)
    out = update(ids, t, c, right, kernel)
    return out.transpose(0, 2, 1, 3)


def solution(mesh):
    fine = Mesh(mesh.devices.reshape(4, 4, 2, 8), ("x", "y", "k", "z"))
    spec = P(None, ROW, None, "z")
    return jax.shard_map(body, mesh=fine, in_specs=(spec,), out_specs=spec, check_vma=False)
```

```python
import jax
import jax.numpy as jnp
from jax import lax
from jax.experimental import pallas as pl
from jax.experimental.pallas import tpu as pltpu
from jax.sharding import Mesh
from jax.sharding import PartitionSpec as P

TILE = 128
TILES = 8
HALF = TILES // 2
WIDTH = TILE * TILES
PANEL = TILE * HALF
GROUP = 16
GRANT = 24 << 20
ROW = ("x", "y", "k")
VMEM = pl.BlockSpec(memory_space=pltpu.VMEM)
SMEM = pl.BlockSpec(memory_space=pltpu.SMEM)


def split(x):
    high = x.astype(jnp.bfloat16)
    rest = x - high.astype(jnp.float32)
    middle = rest.astype(jnp.bfloat16)
    return high, middle, (rest - middle.astype(jnp.float32)).astype(jnp.bfloat16)


def left_terms(parts, axis):
    h, m, l = parts
    return jnp.concatenate([h, h, m, h, l, m], axis)


def right_terms(parts, axis):
    h, m, l = parts
    return jnp.concatenate([h, m, h, l, h, m], axis)


def left_two(parts, axis):
    h, m = parts[:2]
    return jnp.concatenate([h, h, m], axis)


def right_two(parts, axis):
    h, m = parts[:2]
    return jnp.concatenate([h, m, h], axis)


def contract(a, b, da, db):
    return lax.dot_general(a, b, (((da,), (db,)), ((), ())), preferred_element_type=jnp.float32)


def tile(i):
    return pl.ds(pl.multiple_of(i * TILE, TILE), TILE)


def quarter_rows(i, x, d):
    quarter = TILE // 4
    start = i * TILE + lax.rem(x + 4 - d, 4) * quarter
    return pl.ds(pl.multiple_of(start, quarter), quarter)


def spread_row(x, i):
    return jnp.broadcast_to(x[i : i + 1, :], (8, TILE))


def spread_col(x, i):
    return jnp.broadcast_to(x[:, i : i + 1], (8, TILE))


def factor_tile(a_ref, v_ref, hook):
    sub = lax.broadcasted_iota(jnp.int32, (8, TILE), 0)
    lane = lax.broadcasted_iota(jnp.int32, (8, TILE), 1)
    for t in range(TILE // GROUP):
        base = GROUP * t
        total = TILE // 8 - 2 * t
        n = min(4, total)
        rows = [slice(base + 8 * q, base + 8 * q + 8) for q in range(n)]
        a = [a_ref[s, :] for s in rows]
        if t == 0:
            v = [jnp.where(lane == sub + 8 * q, 1.0, 0.0) for q in range(n)]
        else:
            v = [v_ref[s, :] for s in rows]
        cols = [[spread_col(a[q], base + l) for q in range(n)] for l in range(GROUP)]

        def eliminate(j, inverse):
            q0, i = j // 8, j % 8
            m = [
                (cols[j][q] if q > q0 else jnp.where(sub > i, cols[j][q], 0.0)) * inverse
                for q in range(q0, n)
            ]
            for l in range(j + 1, GROUP):
                e = spread_row(cols[l][q0], i)
                for q in range(q0, n):
                    cols[l][q] = cols[l][q] - m[q - q0] * e
            ra, rv = spread_row(a[q0], i), spread_row(v[q0], i)
            for q in range(q0, n):
                a[q] = a[q] - m[q - q0] * ra
                v[q] = v[q] - m[q - q0] * rv

        for j in range(0, GROUP, 2):
            q0, i = j // 8, j % 8
            p = spread_row(cols[j][q0], i)
            g = spread_row(cols[j + 1][q0], i)
            d = spread_row(cols[j + 1][q0], i + 1)
            first = 1.0 / p
            second = p * (1.0 / (p * d - g * g))
            eliminate(j, first)
            eliminate(j + 1, second)
        for q in range(2):
            pivots = cols[8 * q][q]
            for i in range(1, 8):
                pivots = jnp.where(sub == i, cols[8 * q + i][q], pivots)
            scale = lax.rsqrt(pivots)
            a[q] = jnp.where(lane >= sub + base + 8 * q, a[q] * scale, 0.0)
            v[q] = v[q] * scale
        for q in range(n):
            a_ref[rows[q], :] = a[q]
            v_ref[rows[q], :] = v[q]
        if total > n:
            start = base + 8 * n
            done = jnp.concatenate(
                [jnp.concatenate(a[:2], 0), jnp.concatenate(v[:2], 0)], 1
            )
            parts = split(done)
            change = contract(
                left_terms(parts, 0)[:, :TILE], right_terms(parts, 0), 0, 0
            )[start:, :]
            if t == 0:
                shape = (TILE - start, TILE)
                diagonal = lax.broadcasted_iota(jnp.int32, shape, 0) + start
                diagonal = diagonal == lax.broadcasted_iota(jnp.int32, shape, 1)
                v_ref[start:, :] = jnp.where(diagonal, 1.0, 0.0) - change[:, TILE:]
            else:
                v_ref[start:, :] -= change[:, TILE:]
            a_ref[start:, :] -= change[:, :TILE]
        hook(t)


def factor_panel(w_ref, a_ref, v_ref, vp_ref, vs_ref, h_ref, m_ref, l_ref, r_ref):
    w_ref[PANEL : PANEL + TILE, :] = jnp.zeros((TILE, PANEL), jnp.float32)
    a_ref[...] = w_ref[0:TILE, 0:TILE]
    vs_ref[...] = jnp.zeros_like(vs_ref)
    vp_ref[...] = jnp.zeros_like(vp_ref)

    def panel(row, column):
        w_ref[row, :] = contract(vs_ref[...], right_terms(split(w_ref[row, :]), 0), 1, 0)
        w_ref[row, column] = vp_ref[...]

    def step(k, _):
        old = tile(jnp.where(k == 0, HALF, k - 1))
        column = tile(jnp.maximum(k - 1, 0))

        def hook(t):
            if t == 0:
                panel(old, column)
                parts = split(w_ref[old, :])
                h_ref[...], m_ref[...], l_ref[...] = parts
                r_ref[...] = right_terms(parts, 0)
            elif t < HALF:
                i = k + t - 1
                row = tile(jnp.minimum(i, HALF))
                c = tile(jnp.minimum(i, HALF - 1))
                w_ref[row, column] = jnp.zeros((TILE, TILE), jnp.float32)
                left = left_terms((h_ref[:, c], m_ref[:, c], l_ref[:, c]), 0)
                w_ref[row, :] -= contract(left, r_ref[...], 0, 0)

        factor_tile(a_ref, v_ref, hook)
        w_ref[PANEL + TILE :, tile(k)] = a_ref[...]
        vp_ref[...] = v_ref[...]
        vs_ref[...] = left_terms(split(v_ref[...]), 1)
        after = tile(jnp.minimum(k + 1, HALF - 1))
        ahead = contract(vs_ref[...], right_terms(split(w_ref[tile(k), after]), 0), 1, 0)
        parts = split(ahead)
        a_ref[...] = w_ref[after, after] - contract(
            left_terms(parts, 0), right_terms(parts, 0), 0, 0
        )
        return 0

    lax.fori_loop(0, HALF, step, 0)
    panel(tile(HALF - 1), tile(HALF - 1))


def panel_scratch():
    square = pltpu.VMEM((TILE, TILE), jnp.float32)
    part = pltpu.VMEM((TILE, PANEL), jnp.bfloat16)
    return [square, square, square, pltpu.VMEM((TILE, 6 * TILE), jnp.bfloat16)] + [
        part,
        part,
        part,
        pltpu.VMEM((6 * TILE, PANEL), jnp.bfloat16),
    ]


FACTOR = (PANEL + 2 * TILE, PANEL)


def first_kernel(ids_ref, near_ref, far_ref, w_ref, *scratch):
    k, x = ids_ref[3], ids_ref[4]
    for ref, side in ((near_ref, k), (far_ref, 1 - k)):
        for d in range(4):
            for y in range(2):
                rows = quarter_rows(2 * y + side, x, d)
                for j in range(HALF):
                    w_ref[rows, j * TILE : (j + 1) * TILE] = ref[d, y, j]
    factor_panel(w_ref, *scratch)


def first(ids, near, far):
    return pl.pallas_call(
        first_kernel,
        out_shape=jax.ShapeDtypeStruct(FACTOR, jnp.float32),
        in_specs=[SMEM, VMEM, VMEM],
        out_specs=VMEM,
        scratch_shapes=panel_scratch(),
        compiler_params=pltpu.CompilerParams(vmem_limit_bytes=GRANT),
        cost_estimate=pl.CostEstimate(flops=8 << 30, bytes_accessed=4 << 20, transcendentals=0),
        name="first",
    )(ids, near, far)


def factor_second(ids_ref, w0_ref, near_ref, far_ref, x_ref, w_ref, b_ref, *scratch):
    y, k, x = ids_ref[2], ids_ref[3], ids_ref[4]
    for ref, side in ((near_ref, k), (far_ref, 1 - k)):
        for d in range(4):
            for e in range(4):
                rows = quarter_rows(2 * lax.rem(y + 4 - e, 4) + side, x, d)
                for j in range(HALF):
                    b_ref[rows, j * TILE : (j + 1) * TILE] = ref[d, e, j]
    parts = split(b_ref[0:PANEL, :])
    for i in range(HALF):
        n = (i + 1) * TILE
        left = left_terms(split(w0_ref[n - TILE : n, :n]), 1)
        x_ref[n - TILE : n, :] = contract(left, right_terms([p[:n] for p in parts], 0), 1, 0)
    parts = split(x_ref[...])
    right = right_terms(parts, 0)
    for i in range(HALF):
        n = (i + 1) * TILE
        left = left_terms([p[:, n - TILE : n] for p in parts], 0)
        w_ref[n - TILE : n, :] = b_ref[PANEL + n - TILE : PANEL + n, :] - contract(
            left, right, 0, 0
        )
    factor_panel(w_ref, *scratch)


def apply_inverse(ids_ref, own_ref, w0_ref, x_ref, w1_ref, t_ref, c_ref, s_ref):
    row, col = ids_ref[0], ids_ref[1]
    rows = own_ref.shape[1] * TILE
    wide = 2 * TILE
    lower = lax.broadcasted_iota(jnp.int32, (wide, wide), 0) // TILE
    lower = lower >= lax.broadcasted_iota(jnp.int32, (wide, wide), 1) // TILE

    def inverse(w_ref):
        top = jnp.where(lower, w_ref[0:wide, 0:wide], 0.0)
        edge = jnp.where(lower, w_ref[wide:PANEL, wide:PANEL], 0.0)
        bottom = jnp.concatenate([w_ref[wide:PANEL, 0:wide], edge], 1)
        return split(top), split(bottom)

    def times_transpose(a, inv):
        a, (top, bottom) = split(a), inv
        return jnp.concatenate(
            [
                contract(left_two([p[:, :wide] for p in a], 1), right_two(top, 1), 1, 1),
                contract(left_two(a, 1), right_two(bottom, 1), 1, 1),
            ],
            1,
        )

    def times(a, inv):
        a, (top, bottom) = split(a), inv
        below = [p[:, wide:] for p in a]
        left = [jnp.concatenate([b[:, :wide]], 1) for b in bottom]
        both = [jnp.concatenate([t, l], 0) for t, l in zip(top, left)]
        right = [b[:, wide:] for b in bottom]
        return jnp.concatenate(
            [
                contract(left_two(a, 1), right_two(both, 0), 1, 0),
                contract(left_two(below, 1), right_two(right, 0), 1, 0),
            ],
            1,
        )

    def own(first):
        return jnp.concatenate(
            [own_ref[z].reshape(rows, TILE) for z in range(first, first + HALF)], 1
        )

    inv0, inv1 = inverse(w0_ref), inverse(w1_ref)
    x = split(x_ref[...])
    s0 = times_transpose(own(0), inv0)
    s_ref[:, :PANEL] = s0
    rest = own(HALF) - contract(left_two(split(s0), 1), right_two(x, 0), 1, 0)
    s1 = times_transpose(rest, inv1)
    s_ref[:, PANEL:] = s1
    t1 = times(s1, inv1)
    t0 = times(s0 - contract(left_two(split(t1), 1), right_two(x, 1), 1, 1), inv0)
    for start, t in ((0, t0), (PANEL, t1)):
        high = t.astype(jnp.bfloat16)
        t_ref[0, :, start : start + PANEL] = high
        t_ref[1, :, start : start + PANEL] = (t - high.astype(jnp.float32)).astype(jnp.bfloat16)
    c_ref[...] = s_ref[:, tile(col)].reshape(c_ref.shape)

    @pl.when(row < TILES)
    def _():
        c_ref[0] = jnp.zeros((TILE, TILE), jnp.float32)

    for first, w_ref in ((0, w0_ref), (HALF, w1_ref)):

        @pl.when((row >= first) & (row < first + HALF) & (col >= first) & (col <= row))
        def _(first=first, w_ref=w_ref):
            i, j = jnp.clip(col - first, 0, HALF - 1), jnp.clip(row - first, 0, HALF - 1)
            c_ref[0] = w_ref[tile(jnp.where(col == row, HALF + 1, i)), tile(j)].T

    @pl.when((row >= HALF) & (row < TILES) & (col < HALF))
    def _():
        i, j = jnp.clip(col, 0, HALF - 1), jnp.clip(row - HALF, 0, HALF - 1)
        c_ref[0] = x_ref[tile(i), tile(j)].T


def second_kernel(
    ids_ref, w0_ref, near_ref, far_ref, own_hbm, t_hbm, c_hbm,
    t_ref, c_ref, own_ref, sems, x_ref, w1_ref, s_ref, b_ref, *scratch
):
    copy = pltpu.make_async_copy(own_hbm, own_ref, sems.at[0])
    copy.start()
    factor_second(ids_ref, w0_ref, near_ref, far_ref, x_ref, w1_ref, b_ref, *scratch)
    copy.wait()
    apply_inverse(ids_ref, own_ref, w0_ref, x_ref, w1_ref, t_ref, c_ref, s_ref)
    out = [
        pltpu.make_async_copy(t_ref, t_hbm, sems.at[1]),
        pltpu.make_async_copy(c_ref, c_hbm, sems.at[2]),
    ]
    for copy in out:
        copy.start()
    for copy in out:
        copy.wait()


def second(ids, w0, near, far, own):
    rows = own.shape[1] * TILE
    return pl.pallas_call(
        second_kernel,
        out_shape=[
            jax.ShapeDtypeStruct((2, rows, WIDTH), jnp.bfloat16),
            jax.ShapeDtypeStruct((own.shape[1], TILE, TILE), jnp.float32),
        ],
        in_specs=[SMEM, VMEM, VMEM, VMEM, pl.BlockSpec(memory_space=pl.ANY)],
        out_specs=[pl.BlockSpec(memory_space=pltpu.HBM)] * 2,
        scratch_shapes=[
            pltpu.VMEM((2, rows, WIDTH), jnp.bfloat16),
            pltpu.VMEM((own.shape[1], TILE, TILE), jnp.float32),
            pltpu.VMEM(own.shape, jnp.float32),
            pltpu.SemaphoreType.DMA((3,)),
            pltpu.VMEM((PANEL, PANEL), jnp.float32),
            pltpu.VMEM(FACTOR, jnp.float32),
            pltpu.VMEM((rows, WIDTH), jnp.float32),
            pltpu.VMEM((WIDTH, PANEL), jnp.float32),
        ]
        + panel_scratch(),
        compiler_params=pltpu.CompilerParams(vmem_limit_bytes=GRANT),
        cost_estimate=pl.CostEstimate(flops=16 << 30, bytes_accessed=8 << 20, transcendentals=0),
        name="second",
    )(ids, w0, near, far, own)


def update_kernel(ids_ref, t_ref, c_ref, *refs):
    *right_refs, k_ref, o_ref = refs
    n = len(right_refs)
    right = jnp.concatenate(
        [
            jnp.concatenate([ref[x, r, 0] for r in range(TILES) for x in range(4)], 0)
            for ref in right_refs
        ],
        1,
    )
    high = right.astype(jnp.bfloat16)
    low = (right - high.astype(jnp.float32)).astype(jnp.bfloat16)
    left = jnp.concatenate([t_ref[0], t_ref[0], t_ref[1]], 1)
    product = contract(left, jnp.concatenate([high, low, high], 0), 1, 0)
    product = product.reshape(-1, TILE, n * TILE)
    for i in range(n):
        o_ref[:, i] = k_ref[:, i] - product[:, :, i * TILE : (i + 1) * TILE]

    @pl.when(ids_ref[0] < TILES)
    def _():
        o_ref[0] = jnp.zeros(o_ref.shape[1:], jnp.float32)

    @pl.when(pl.program_id(0) == 0)
    def _():
        o_ref[:, 0] = c_ref[...]


def update(ids, t, c, right, kernel):
    tiles, columns = kernel.shape[:2]
    n = 4
    block = pl.BlockSpec((tiles, n, TILE, TILE), lambda j: (0, j, 0, 0))

    def piece(i):
        return pl.BlockSpec(
            (4, TILES, 1, TILE // 4, TILE),
            lambda j: (0, 0, jnp.maximum(n * j + i - 1, 0), 0, 0),
        )

    return pl.pallas_call(
        update_kernel,
        grid=(columns // n,),
        out_shape=jax.ShapeDtypeStruct(kernel.shape, jnp.float32),
        in_specs=[SMEM, VMEM, VMEM] + [piece(i) for i in range(n)] + [block],
        out_specs=block,
        compiler_params=pltpu.CompilerParams(vmem_limit_bytes=60 << 20),
        name="update",
    )(ids, t, c, *[right] * n, kernel)


def swap(x):
    return lax.ppermute(x, "k", [(0, 1), (1, 0)])


def send(x, axis, pairs):
    return lax.ppermute(x, axis, pairs)


def around(block, axis):
    n = lax.axis_size(axis)
    return [block] + [send(block, axis, [(i, (i + d) % n) for i in range(n)]) for d in range(1, n)]


def gather_z(block):
    n = lax.axis_size("z")
    k, z = lax.axis_index("k"), lax.axis_index("z")
    pair = jnp.stack([block, swap(block)])
    parts = []
    for d in (1, 2, 3):
        up = [(i, (i + d) % n) for i in range(n)]
        down = [(n + i, n + (i - d) % n) for i in range(n)]
        parts.append(send(pair, ("k", "z"), up + down))
    far = send(block, "z", [(i, (i + n // 2) % n) for i in range(n)])
    parts, far = lax.optimization_barrier((parts, far))
    mine = jnp.stack([p[0] for p in parts])
    other = swap(jnp.stack([p[1] for p in parts]))
    below = jnp.where(k == 0, mine, other)
    above = jnp.where(k == 0, other, mine)
    ring = jnp.concatenate([block[None], above, far[None], below[::-1]])
    return lax.dynamic_slice_in_dim(jnp.concatenate([ring, ring]), (n - z) % n, n, 0)


def body(kernel):
    kernel = kernel.transpose(0, 2, 1, 3)
    x = lax.axis_index("x")
    y = lax.axis_index("y")
    places = (ROW, "z", "y", "k", "x")
    ids = jnp.stack([lax.axis_index(a) for a in places]).astype(jnp.int32)
    mine, kernel = lax.optimization_barrier((kernel[:, 0], kernel))
    own = lax.all_gather(mine, "z")

    quarters = kernel[0].reshape(-1, 4, TILE // 4, TILE)
    quarter = quarters[:, 0]
    for d in (1, 3, 2):
        quarter = jnp.where(x == d, send(quarters[:, d], "x", [(0, d)]), quarter)
    right = lax.all_gather(quarter[1:], ROW)
    right = right.reshape(4, TILES, -1, TILE // 4, TILE)

    strips = jnp.stack(around(gather_z(quarter[0]), "y"))
    top = [lax.dynamic_index_in_dim(strips, (y + 4 - i) % 4, 0, False)[:HALF] for i in range(2)]
    near = jnp.stack(around(jnp.stack(top), "x"))
    near, rest, own = lax.optimization_barrier((near, strips[:, HALF:], own))
    far = swap(near)
    parts = around(rest, "x")
    w0 = first(ids, near, far)
    w0, parts = lax.optimization_barrier((w0, parts))
    more = jnp.stack(parts)
    t, c = second(ids, w0, more, swap(more), own)
    out = update(ids, t, c, right, kernel)
    return out.transpose(0, 2, 1, 3)


def solution(mesh):
    fine = Mesh(mesh.devices.reshape(4, 4, 2, 8), ("x", "y", "k", "z"))
    spec = P(None, ROW, None, "z")
    return jax.shard_map(body, mesh=fine, in_specs=(spec,), out_specs=spec, check_vma=False)
```

```python
import jax
import jax.numpy as jnp
from jax import lax
from jax.experimental import pallas as pl
from jax.experimental.pallas import tpu as pltpu
from jax.sharding import Mesh
from jax.sharding import PartitionSpec as P

TILE = 128
TILES = 8
HALF = TILES // 2
WIDTH = TILE * TILES
PANEL = TILE * HALF
GROUP = 16
GRANT = 24 << 20
ROW = ("x", "y", "k")
VMEM = pl.BlockSpec(memory_space=pltpu.VMEM)
SMEM = pl.BlockSpec(memory_space=pltpu.SMEM)


def split(x):
    high = x.astype(jnp.bfloat16)
    rest = x - high.astype(jnp.float32)
    middle = rest.astype(jnp.bfloat16)
    return high, middle, (rest - middle.astype(jnp.float32)).astype(jnp.bfloat16)


def left_terms(parts, axis):
    h, m, l = parts
    return jnp.concatenate([h, h, m, h, l, m], axis)


def right_terms(parts, axis):
    h, m, l = parts
    return jnp.concatenate([h, m, h, l, h, m], axis)


def left_two(parts, axis):
    h, m = parts[:2]
    return jnp.concatenate([h, h, m], axis)


def right_two(parts, axis):
    h, m = parts[:2]
    return jnp.concatenate([h, m, h], axis)


def contract(a, b, da, db):
    return lax.dot_general(a, b, (((da,), (db,)), ((), ())), preferred_element_type=jnp.float32)


def tile(i):
    return pl.ds(pl.multiple_of(i * TILE, TILE), TILE)


def quarter_rows(i, x, d):
    quarter = TILE // 4
    start = i * TILE + lax.rem(x + 4 - d, 4) * quarter
    return pl.ds(pl.multiple_of(start, quarter), quarter)


def spread_row(x, i):
    return jnp.broadcast_to(x[i : i + 1, :], (8, TILE))


def spread_col(x, i):
    return jnp.broadcast_to(x[:, i : i + 1], (8, TILE))


def factor_tile(a_ref, v_ref, hook):
    sub = lax.broadcasted_iota(jnp.int32, (8, TILE), 0)
    lane = lax.broadcasted_iota(jnp.int32, (8, TILE), 1)
    for t in range(TILE // GROUP):
        base = GROUP * t
        total = TILE // 8 - 2 * t
        n = min(4, total)
        rows = [slice(base + 8 * q, base + 8 * q + 8) for q in range(n)]
        a = [a_ref[s, :] for s in rows]
        if t == 0:
            v = [jnp.where(lane == sub + 8 * q, 1.0, 0.0) for q in range(n)]
        else:
            v = [v_ref[s, :] for s in rows]
        cols = [[spread_col(a[q], base + l) for q in range(n)] for l in range(GROUP)]

        def eliminate(j, inverse):
            q0, i = j // 8, j % 8
            m = [
                (cols[j][q] if q > q0 else jnp.where(sub > i, cols[j][q], 0.0)) * inverse
                for q in range(q0, n)
            ]
            for l in range(j + 1, GROUP):
                e = spread_row(cols[l][q0], i)
                for q in range(q0, n):
                    cols[l][q] = cols[l][q] - m[q - q0] * e
            ra, rv = spread_row(a[q0], i), spread_row(v[q0], i)
            for q in range(q0, n):
                a[q] = a[q] - m[q - q0] * ra
                v[q] = v[q] - m[q - q0] * rv

        for j in range(0, GROUP, 2):
            q0, i = j // 8, j % 8
            p = spread_row(cols[j][q0], i)
            g = spread_row(cols[j + 1][q0], i)
            d = spread_row(cols[j + 1][q0], i + 1)
            first = 1.0 / p
            second = 1.0 / (d - g * first * g)
            eliminate(j, first)
            eliminate(j + 1, second)
        for q in range(2):
            pivots = cols[8 * q][q]
            for i in range(1, 8):
                pivots = jnp.where(sub == i, cols[8 * q + i][q], pivots)
            scale = lax.rsqrt(pivots)
            a[q] = jnp.where(lane >= sub + base + 8 * q, a[q] * scale, 0.0)
            v[q] = v[q] * scale
        for q in range(n):
            a_ref[rows[q], :] = a[q]
            v_ref[rows[q], :] = v[q]
        if total > n:
            start = base + 8 * n
            done = jnp.concatenate(
                [jnp.concatenate(a[:2], 0), jnp.concatenate(v[:2], 0)], 1
            )
            parts = split(done)
            change = contract(
                left_terms(parts, 0)[:, :TILE], right_terms(parts, 0), 0, 0
            )[start:, :]
            if t == 0:
                shape = (TILE - start, TILE)
                diagonal = lax.broadcasted_iota(jnp.int32, shape, 0) + start
                diagonal = diagonal == lax.broadcasted_iota(jnp.int32, shape, 1)
                v_ref[start:, :] = jnp.where(diagonal, 1.0, 0.0) - change[:, TILE:]
            else:
                v_ref[start:, :] -= change[:, TILE:]
            a_ref[start:, :] -= change[:, :TILE]
        hook(t)


def factor_panel(w_ref, a_ref, v_ref, vp_ref, vs_ref, h_ref, m_ref, l_ref, r_ref):
    w_ref[PANEL : PANEL + TILE, :] = jnp.zeros((TILE, PANEL), jnp.float32)
    a_ref[...] = w_ref[0:TILE, 0:TILE]
    vs_ref[...] = jnp.zeros_like(vs_ref)
    vp_ref[...] = jnp.zeros_like(vp_ref)

    def panel(row, column):
        w_ref[row, :] = contract(vs_ref[...], right_terms(split(w_ref[row, :]), 0), 1, 0)
        w_ref[row, column] = vp_ref[...]

    def step(k, _):
        old = tile(jnp.where(k == 0, HALF, k - 1))
        column = tile(jnp.maximum(k - 1, 0))

        def hook(t):
            if t == 0:
                panel(old, column)
                parts = split(w_ref[old, :])
                h_ref[...], m_ref[...], l_ref[...] = parts
                r_ref[...] = right_terms(parts, 0)
            elif t < HALF:
                i = k + t - 1
                row = tile(jnp.minimum(i, HALF))
                c = tile(jnp.minimum(i, HALF - 1))
                w_ref[row, column] = jnp.zeros((TILE, TILE), jnp.float32)
                left = left_terms((h_ref[:, c], m_ref[:, c], l_ref[:, c]), 0)
                w_ref[row, :] -= contract(left, r_ref[...], 0, 0)

        factor_tile(a_ref, v_ref, hook)
        w_ref[PANEL + TILE :, tile(k)] = a_ref[...]
        vp_ref[...] = v_ref[...]
        vs_ref[...] = left_terms(split(v_ref[...]), 1)
        after = tile(jnp.minimum(k + 1, HALF - 1))
        ahead = contract(vs_ref[...], right_terms(split(w_ref[tile(k), after]), 0), 1, 0)
        parts = split(ahead)
        a_ref[...] = w_ref[after, after] - contract(
            left_terms(parts, 0), right_terms(parts, 0), 0, 0
        )
        return 0

    lax.fori_loop(0, HALF, step, 0)
    panel(tile(HALF - 1), tile(HALF - 1))


def panel_scratch():
    square = pltpu.VMEM((TILE, TILE), jnp.float32)
    part = pltpu.VMEM((TILE, PANEL), jnp.bfloat16)
    return [square, square, square, pltpu.VMEM((TILE, 6 * TILE), jnp.bfloat16)] + [
        part,
        part,
        part,
        pltpu.VMEM((6 * TILE, PANEL), jnp.bfloat16),
    ]


FACTOR = (PANEL + 2 * TILE, PANEL)


def first_kernel(ids_ref, near_ref, far_ref, w_ref, *scratch):
    k, x = ids_ref[3], ids_ref[4]
    for ref, side in ((near_ref, k), (far_ref, 1 - k)):
        for d in range(4):
            for y in range(2):
                rows = quarter_rows(2 * y + side, x, d)
                for j in range(HALF):
                    w_ref[rows, j * TILE : (j + 1) * TILE] = ref[d, y, j]
    factor_panel(w_ref, *scratch)


def first(ids, near, far):
    return pl.pallas_call(
        first_kernel,
        out_shape=jax.ShapeDtypeStruct(FACTOR, jnp.float32),
        in_specs=[SMEM, VMEM, VMEM],
        out_specs=VMEM,
        scratch_shapes=panel_scratch(),
        compiler_params=pltpu.CompilerParams(vmem_limit_bytes=GRANT),
        cost_estimate=pl.CostEstimate(flops=8 << 30, bytes_accessed=4 << 20, transcendentals=0),
        name="first",
    )(ids, near, far)


def factor_second(ids_ref, w0_ref, near_ref, far_ref, x_ref, w_ref, b_ref, *scratch):
    y, k, x = ids_ref[2], ids_ref[3], ids_ref[4]
    for ref, side in ((near_ref, k), (far_ref, 1 - k)):
        for d in range(4):
            for e in range(4):
                rows = quarter_rows(2 * lax.rem(y + 4 - e, 4) + side, x, d)
                for j in range(HALF):
                    b_ref[rows, j * TILE : (j + 1) * TILE] = ref[d, e, j]
    parts = split(b_ref[0:PANEL, :])
    for i in range(HALF):
        n = (i + 1) * TILE
        left = left_terms(split(w0_ref[n - TILE : n, :n]), 1)
        x_ref[n - TILE : n, :] = contract(left, right_terms([p[:n] for p in parts], 0), 1, 0)
    parts = split(x_ref[...])
    right = right_terms(parts, 0)
    for i in range(HALF):
        n = (i + 1) * TILE
        left = left_terms([p[:, n - TILE : n] for p in parts], 0)
        w_ref[n - TILE : n, :] = b_ref[PANEL + n - TILE : PANEL + n, :] - contract(
            left, right, 0, 0
        )
    factor_panel(w_ref, *scratch)


def apply_inverse(ids_ref, own_ref, w0_ref, x_ref, w1_ref, t_ref, c_ref, s_ref):
    row, col = ids_ref[0], ids_ref[1]
    rows = own_ref.shape[1] * TILE
    wide = 2 * TILE
    lower = lax.broadcasted_iota(jnp.int32, (wide, wide), 0) // TILE
    lower = lower >= lax.broadcasted_iota(jnp.int32, (wide, wide), 1) // TILE

    def inverse(w_ref):
        top = jnp.where(lower, w_ref[0:wide, 0:wide], 0.0)
        edge = jnp.where(lower, w_ref[wide:PANEL, wide:PANEL], 0.0)
        bottom = jnp.concatenate([w_ref[wide:PANEL, 0:wide], edge], 1)
        return split(top), split(bottom)

    def times_transpose(a, inv):
        a, (top, bottom) = split(a), inv
        return jnp.concatenate(
            [
                contract(left_two([p[:, :wide] for p in a], 1), right_two(top, 1), 1, 1),
                contract(left_two(a, 1), right_two(bottom, 1), 1, 1),
            ],
            1,
        )

    def times(a, inv):
        a, (top, bottom) = split(a), inv
        below = [p[:, wide:] for p in a]
        left = [jnp.concatenate([b[:, :wide]], 1) for b in bottom]
        both = [jnp.concatenate([t, l], 0) for t, l in zip(top, left)]
        right = [b[:, wide:] for b in bottom]
        return jnp.concatenate(
            [
                contract(left_two(a, 1), right_two(both, 0), 1, 0),
                contract(left_two(below, 1), right_two(right, 0), 1, 0),
            ],
            1,
        )

    def own(first):
        return jnp.concatenate(
            [own_ref[z].reshape(rows, TILE) for z in range(first, first + HALF)], 1
        )

    inv0, inv1 = inverse(w0_ref), inverse(w1_ref)
    x = split(x_ref[...])
    s0 = times_transpose(own(0), inv0)
    s_ref[:, :PANEL] = s0
    rest = own(HALF) - contract(left_two(split(s0), 1), right_two(x, 0), 1, 0)
    s1 = times_transpose(rest, inv1)
    s_ref[:, PANEL:] = s1
    t1 = times(s1, inv1)
    t0 = times(s0 - contract(left_two(split(t1), 1), right_two(x, 1), 1, 1), inv0)
    for start, t in ((0, t0), (PANEL, t1)):
        high = t.astype(jnp.bfloat16)
        t_ref[0, :, start : start + PANEL] = high
        t_ref[1, :, start : start + PANEL] = (t - high.astype(jnp.float32)).astype(jnp.bfloat16)
    c_ref[...] = s_ref[:, tile(col)].reshape(c_ref.shape)

    @pl.when(row < TILES)
    def _():
        c_ref[0] = jnp.zeros((TILE, TILE), jnp.float32)

    for first, w_ref in ((0, w0_ref), (HALF, w1_ref)):

        @pl.when((row >= first) & (row < first + HALF) & (col >= first) & (col <= row))
        def _(first=first, w_ref=w_ref):
            i, j = jnp.clip(col - first, 0, HALF - 1), jnp.clip(row - first, 0, HALF - 1)
            c_ref[0] = w_ref[tile(jnp.where(col == row, HALF + 1, i)), tile(j)].T

    @pl.when((row >= HALF) & (row < TILES) & (col < HALF))
    def _():
        i, j = jnp.clip(col, 0, HALF - 1), jnp.clip(row - HALF, 0, HALF - 1)
        c_ref[0] = x_ref[tile(i), tile(j)].T


def second_kernel(
    ids_ref, w0_ref, near_ref, far_ref, own_hbm, t_hbm, c_hbm,
    t_ref, c_ref, own_ref, sems, x_ref, w1_ref, s_ref, b_ref, *scratch
):
    copy = pltpu.make_async_copy(own_hbm, own_ref, sems.at[0])
    copy.start()
    factor_second(ids_ref, w0_ref, near_ref, far_ref, x_ref, w1_ref, b_ref, *scratch)
    copy.wait()
    apply_inverse(ids_ref, own_ref, w0_ref, x_ref, w1_ref, t_ref, c_ref, s_ref)
    out = [
        pltpu.make_async_copy(t_ref, t_hbm, sems.at[1]),
        pltpu.make_async_copy(c_ref, c_hbm, sems.at[2]),
    ]
    for copy in out:
        copy.start()
    for copy in out:
        copy.wait()


def second(ids, w0, near, far, own):
    rows = own.shape[1] * TILE
    return pl.pallas_call(
        second_kernel,
        out_shape=[
            jax.ShapeDtypeStruct((2, rows, WIDTH), jnp.bfloat16),
            jax.ShapeDtypeStruct((own.shape[1], TILE, TILE), jnp.float32),
        ],
        in_specs=[SMEM, VMEM, VMEM, VMEM, pl.BlockSpec(memory_space=pl.ANY)],
        out_specs=[pl.BlockSpec(memory_space=pltpu.HBM)] * 2,
        scratch_shapes=[
            pltpu.VMEM((2, rows, WIDTH), jnp.bfloat16),
            pltpu.VMEM((own.shape[1], TILE, TILE), jnp.float32),
            pltpu.VMEM(own.shape, jnp.float32),
            pltpu.SemaphoreType.DMA((3,)),
            pltpu.VMEM((PANEL, PANEL), jnp.float32),
            pltpu.VMEM(FACTOR, jnp.float32),
            pltpu.VMEM((rows, WIDTH), jnp.float32),
            pltpu.VMEM((WIDTH, PANEL), jnp.float32),
        ]
        + panel_scratch(),
        compiler_params=pltpu.CompilerParams(vmem_limit_bytes=GRANT),
        cost_estimate=pl.CostEstimate(flops=16 << 30, bytes_accessed=8 << 20, transcendentals=0),
        name="second",
    )(ids, w0, near, far, own)


def update_kernel(ids_ref, t_ref, c_ref, *refs):
    *right_refs, k_ref, o_ref = refs
    n = len(right_refs)
    right = jnp.concatenate(
        [
            jnp.concatenate([ref[x, r, 0] for r in range(TILES) for x in range(4)], 0)
            for ref in right_refs
        ],
        1,
    )
    high = right.astype(jnp.bfloat16)
    low = (right - high.astype(jnp.float32)).astype(jnp.bfloat16)
    left = jnp.concatenate([t_ref[0], t_ref[0], t_ref[1]], 1)
    product = contract(left, jnp.concatenate([high, low, high], 0), 1, 0)
    product = product.reshape(-1, TILE, n * TILE)
    for i in range(n):
        o_ref[:, i] = k_ref[:, i] - product[:, :, i * TILE : (i + 1) * TILE]

    @pl.when(ids_ref[0] < TILES)
    def _():
        o_ref[0] = jnp.zeros(o_ref.shape[1:], jnp.float32)

    @pl.when(pl.program_id(0) == 0)
    def _():
        o_ref[:, 0] = c_ref[...]


def update(ids, t, c, right, kernel):
    tiles, columns = kernel.shape[:2]
    n = 4
    block = pl.BlockSpec((tiles, n, TILE, TILE), lambda j: (0, j, 0, 0))

    def piece(i):
        return pl.BlockSpec(
            (4, TILES, 1, TILE // 4, TILE),
            lambda j: (0, 0, jnp.maximum(n * j + i - 1, 0), 0, 0),
        )

    return pl.pallas_call(
        update_kernel,
        grid=(columns // n,),
        out_shape=jax.ShapeDtypeStruct(kernel.shape, jnp.float32),
        in_specs=[SMEM, VMEM, VMEM] + [piece(i) for i in range(n)] + [block],
        out_specs=block,
        compiler_params=pltpu.CompilerParams(vmem_limit_bytes=60 << 20),
        name="update",
    )(ids, t, c, *[right] * n, kernel)


def swap(x):
    return lax.ppermute(x, "k", [(0, 1), (1, 0)])


def send(x, axis, pairs):
    return lax.ppermute(x, axis, pairs)


def around(block, axis):
    n = lax.axis_size(axis)
    return [block] + [send(block, axis, [(i, (i + d) % n) for i in range(n)]) for d in range(1, n)]


def gather_z(block):
    n = lax.axis_size("z")
    k, z = lax.axis_index("k"), lax.axis_index("z")
    pair = jnp.stack([block, swap(block)])
    parts = []
    for d in (1, 2, 3):
        up = [(i, (i + d) % n) for i in range(n)]
        down = [(n + i, n + (i - d) % n) for i in range(n)]
        parts.append(send(pair, ("k", "z"), up + down))
    far = send(block, "z", [(i, (i + n // 2) % n) for i in range(n)])
    parts, far = lax.optimization_barrier((parts, far))
    mine = jnp.stack([p[0] for p in parts])
    other = swap(jnp.stack([p[1] for p in parts]))
    below = jnp.where(k == 0, mine, other)
    above = jnp.where(k == 0, other, mine)
    ring = jnp.concatenate([block[None], above, far[None], below[::-1]])
    return lax.dynamic_slice_in_dim(jnp.concatenate([ring, ring]), (n - z) % n, n, 0)


def body(kernel):
    kernel = kernel.transpose(0, 2, 1, 3)
    x = lax.axis_index("x")
    y = lax.axis_index("y")
    places = (ROW, "z", "y", "k", "x")
    ids = jnp.stack([lax.axis_index(a) for a in places]).astype(jnp.int32)
    mine, kernel = lax.optimization_barrier((kernel[:, 0], kernel))
    own = lax.all_gather(mine, "z")

    quarters = kernel[0].reshape(-1, 4, TILE // 4, TILE)
    quarter = quarters[:, 0]
    for d in (1, 3, 2):
        quarter = jnp.where(x == d, send(quarters[:, d], "x", [(0, d)]), quarter)
    right = lax.all_gather(quarter[1:], ROW)
    right = right.reshape(4, TILES, -1, TILE // 4, TILE)

    strips = jnp.stack(around(gather_z(quarter[0]), "y"))
    top = [lax.dynamic_index_in_dim(strips, (y + 4 - i) % 4, 0, False)[:HALF] for i in range(2)]
    near = jnp.stack(around(jnp.stack(top), "x"))
    near, rest, own = lax.optimization_barrier((near, strips[:, HALF:], own))
    far = swap(near)
    parts = around(rest, "x")
    w0 = first(ids, near, far)
    w0, parts = lax.optimization_barrier((w0, parts))
    more = jnp.stack(parts)
    t, c = second(ids, w0, more, swap(more), own)
    out = update(ids, t, c, right, kernel)
    return out.transpose(0, 2, 1, 3)


def solution(mesh):
    fine = Mesh(mesh.devices.reshape(4, 4, 2, 8), ("x", "y", "k", "z"))
    spec = P(None, ROW, None, "z")
    return jax.shard_map(body, mesh=fine, in_specs=(spec,), out_specs=spec, check_vma=False)
```

```python
import jax
import jax.numpy as jnp
from jax import lax
from jax.experimental import pallas as pl
from jax.experimental.pallas import tpu as pltpu
from jax.sharding import Mesh
from jax.sharding import PartitionSpec as P

TILE = 128
TILES = 8
HALF = TILES // 2
WIDTH = TILE * TILES
PANEL = TILE * HALF
GROUP = 16
GRANT = 24 << 20
ROW = ("x", "y", "k")
VMEM = pl.BlockSpec(memory_space=pltpu.VMEM)
SMEM = pl.BlockSpec(memory_space=pltpu.SMEM)


def split(x):
    high = x.astype(jnp.bfloat16)
    rest = x - high.astype(jnp.float32)
    middle = rest.astype(jnp.bfloat16)
    return high, middle, (rest - middle.astype(jnp.float32)).astype(jnp.bfloat16)


def left_terms(parts, axis):
    h, m, l = parts
    return jnp.concatenate([h, h, m, h, l, m], axis)


def right_terms(parts, axis):
    h, m, l = parts
    return jnp.concatenate([h, m, h, l, h, m], axis)


def left_two(parts, axis):
    h, m = parts[:2]
    return jnp.concatenate([h, h, m], axis)


def right_two(parts, axis):
    h, m = parts[:2]
    return jnp.concatenate([h, m, h], axis)


def contract(a, b, da, db):
    return lax.dot_general(a, b, (((da,), (db,)), ((), ())), preferred_element_type=jnp.float32)


def tile(i):
    return pl.ds(pl.multiple_of(i * TILE, TILE), TILE)


def quarter_rows(i, x, d):
    quarter = TILE // 4
    start = i * TILE + lax.rem(x + 4 - d, 4) * quarter
    return pl.ds(pl.multiple_of(start, quarter), quarter)


def spread_row(x, i):
    return jnp.broadcast_to(x[i : i + 1, :], (8, TILE))


def spread_col(x, i):
    return jnp.broadcast_to(x[:, i : i + 1], (8, TILE))


def factor_tile(a_ref, v_ref, hook):
    sub = lax.broadcasted_iota(jnp.int32, (8, TILE), 0)
    lane = lax.broadcasted_iota(jnp.int32, (8, TILE), 1)
    for t in range(TILE // GROUP):
        base = GROUP * t
        total = TILE // 8 - 2 * t
        n = min(4, total)
        rows = [slice(base + 8 * q, base + 8 * q + 8) for q in range(n)]
        a = [a_ref[s, :] for s in rows]
        if t == 0:
            v = [jnp.where(lane == sub + 8 * q, 1.0, 0.0) for q in range(n)]
        else:
            v = [v_ref[s, :] for s in rows]
        cols = [[spread_col(a[q], base + l) for q in range(n)] for l in range(GROUP)]

        def eliminate(j, inverse):
            q0, i = j // 8, j % 8
            m = [
                (cols[j][q] if q > q0 else jnp.where(sub > i, cols[j][q], 0.0)) * inverse
                for q in range(q0, n)
            ]
            for l in range(j + 1, GROUP):
                e = spread_row(cols[l][q0], i)
                for q in range(q0, n):
                    cols[l][q] = cols[l][q] - m[q - q0] * e
            ra, rv = spread_row(a[q0], i), spread_row(v[q0], i)
            for q in range(q0, n):
                a[q] = a[q] - m[q - q0] * ra
                v[q] = v[q] - m[q - q0] * rv

        for j in range(0, GROUP, 2):
            q0, i = j // 8, j % 8
            p = spread_row(cols[j][q0], i)
            g = spread_row(cols[j + 1][q0], i)
            d = spread_row(cols[j + 1][q0], i + 1)
            first = 1.0 / p
            second = 1.0 / (d - g * first * g)
            eliminate(j, first)
            eliminate(j + 1, second)
        for q in range(2):
            pivots = cols[8 * q][q]
            for i in range(1, 8):
                pivots = jnp.where(sub == i, cols[8 * q + i][q], pivots)
            scale = lax.rsqrt(pivots)
            a[q] = jnp.where(lane >= sub + base + 8 * q, a[q] * scale, 0.0)
            v[q] = v[q] * scale
        for q in range(n):
            a_ref[rows[q], :] = a[q]
            v_ref[rows[q], :] = v[q]
        if total > n:
            start = base + 8 * n
            done = jnp.concatenate(
                [jnp.concatenate(a[:2], 0), jnp.concatenate(v[:2], 0)], 1
            )
            parts = split(done)
            change = contract(
                left_terms(parts, 0)[:, :TILE], right_terms(parts, 0), 0, 0
            )[start:, :]
            if t == 0:
                shape = (TILE - start, TILE)
                diagonal = lax.broadcasted_iota(jnp.int32, shape, 0) + start
                diagonal = diagonal == lax.broadcasted_iota(jnp.int32, shape, 1)
                v_ref[start:, :] = jnp.where(diagonal, 1.0, 0.0) - change[:, TILE:]
            else:
                v_ref[start:, :] -= change[:, TILE:]
            a_ref[start:, :] -= change[:, :TILE]
        hook(t)


def factor_panel(w_ref, a_ref, v_ref, vp_ref, vs_ref, h_ref, m_ref, l_ref, r_ref):
    w_ref[PANEL : PANEL + TILE, :] = jnp.zeros((TILE, PANEL), jnp.float32)
    a_ref[...] = w_ref[0:TILE, 0:TILE]
    vs_ref[...] = jnp.zeros_like(vs_ref)
    vp_ref[...] = jnp.zeros_like(vp_ref)

    def panel(row, column):
        w_ref[row, :] = contract(vs_ref[...], right_terms(split(w_ref[row, :]), 0), 1, 0)
        w_ref[row, column] = vp_ref[...]

    def step(k, _):
        old = tile(jnp.where(k == 0, HALF, k - 1))
        column = tile(jnp.maximum(k - 1, 0))

        def hook(t):
            if t == 0:
                panel(old, column)
                parts = split(w_ref[old, :])
                h_ref[...], m_ref[...], l_ref[...] = parts
                r_ref[...] = right_terms(parts, 0)
            elif t < HALF:
                i = k + t - 1
                row = tile(jnp.minimum(i, HALF))
                c = tile(jnp.minimum(i, HALF - 1))
                w_ref[row, column] = jnp.zeros((TILE, TILE), jnp.float32)
                left = left_terms((h_ref[:, c], m_ref[:, c], l_ref[:, c]), 0)
                w_ref[row, :] -= contract(left, r_ref[...], 0, 0)

        factor_tile(a_ref, v_ref, hook)
        w_ref[PANEL + TILE :, tile(k)] = a_ref[...]
        vp_ref[...] = v_ref[...]
        vs_ref[...] = left_terms(split(v_ref[...]), 1)
        after = tile(jnp.minimum(k + 1, HALF - 1))
        ahead = contract(vs_ref[...], right_terms(split(w_ref[tile(k), after]), 0), 1, 0)
        parts = split(ahead)
        a_ref[...] = w_ref[after, after] - contract(
            left_terms(parts, 0), right_terms(parts, 0), 0, 0
        )
        return 0

    lax.fori_loop(0, HALF, step, 0)
    panel(tile(HALF - 1), tile(HALF - 1))


def panel_scratch():
    square = pltpu.VMEM((TILE, TILE), jnp.float32)
    part = pltpu.VMEM((TILE, PANEL), jnp.bfloat16)
    return [square, square, square, pltpu.VMEM((TILE, 6 * TILE), jnp.bfloat16)] + [
        part,
        part,
        part,
        pltpu.VMEM((6 * TILE, PANEL), jnp.bfloat16),
    ]


FACTOR = (PANEL + 2 * TILE, PANEL)


def first_kernel(ids_ref, near_ref, far_ref, w_ref, *scratch):
    k, x = ids_ref[3], ids_ref[4]
    for ref, side in ((near_ref, k), (far_ref, 1 - k)):
        for d in range(4):
            for y in range(2):
                rows = quarter_rows(2 * y + side, x, d)
                for j in range(HALF):
                    w_ref[rows, j * TILE : (j + 1) * TILE] = ref[d, y, j]
    factor_panel(w_ref, *scratch)


def first(ids, near, far):
    return pl.pallas_call(
        first_kernel,
        out_shape=jax.ShapeDtypeStruct(FACTOR, jnp.float32),
        in_specs=[SMEM, VMEM, VMEM],
        out_specs=VMEM,
        scratch_shapes=panel_scratch(),
        compiler_params=pltpu.CompilerParams(vmem_limit_bytes=GRANT),
        cost_estimate=pl.CostEstimate(flops=8 << 30, bytes_accessed=4 << 20, transcendentals=0),
        name="first",
    )(ids, near, far)


def factor_second(ids_ref, w0_ref, near_ref, far_ref, x_ref, w_ref, b_ref, *scratch):
    y, k, x = ids_ref[2], ids_ref[3], ids_ref[4]
    for ref, side in ((near_ref, k), (far_ref, 1 - k)):
        for d in range(4):
            for e in range(4):
                rows = quarter_rows(2 * lax.rem(y + 4 - e, 4) + side, x, d)
                for j in range(HALF):
                    b_ref[rows, j * TILE : (j + 1) * TILE] = ref[d, e, j]
    parts = split(b_ref[0:PANEL, :])
    for i in range(HALF):
        n = (i + 1) * TILE
        left = left_terms(split(w0_ref[n - TILE : n, :n]), 1)
        x_ref[n - TILE : n, :] = contract(left, right_terms([p[:n] for p in parts], 0), 1, 0)
    parts = split(x_ref[...])
    right = right_terms(parts, 0)
    for i in range(HALF):
        n = (i + 1) * TILE
        left = left_terms([p[:, n - TILE : n] for p in parts], 0)
        w_ref[n - TILE : n, :] = b_ref[PANEL + n - TILE : PANEL + n, :] - contract(
            left, right, 0, 0
        )
    factor_panel(w_ref, *scratch)


def apply_inverse(ids_ref, own_ref, w0_ref, x_ref, w1_ref, t_ref, c_ref, s_ref):
    row, col = ids_ref[0], ids_ref[1]
    rows = own_ref.shape[1] * TILE
    wide = 2 * TILE
    lower = lax.broadcasted_iota(jnp.int32, (wide, wide), 0) // TILE
    lower = lower >= lax.broadcasted_iota(jnp.int32, (wide, wide), 1) // TILE

    def inverse(w_ref):
        top = jnp.where(lower, w_ref[0:wide, 0:wide], 0.0)
        edge = jnp.where(lower, w_ref[wide:PANEL, wide:PANEL], 0.0)
        bottom = jnp.concatenate([w_ref[wide:PANEL, 0:wide], edge], 1)
        return split(top), split(bottom)

    def times_transpose(a, inv):
        a, (top, bottom) = split(a), inv
        return jnp.concatenate(
            [
                contract(left_two([p[:, :wide] for p in a], 1), right_two(top, 1), 1, 1),
                contract(left_two(a, 1), right_two(bottom, 1), 1, 1),
            ],
            1,
        )

    def times(a, inv):
        a, (top, bottom) = split(a), inv
        below = [p[:, wide:] for p in a]
        left = [jnp.concatenate([b[:, :wide]], 1) for b in bottom]
        both = [jnp.concatenate([t, l], 0) for t, l in zip(top, left)]
        right = [b[:, wide:] for b in bottom]
        return jnp.concatenate(
            [
                contract(left_two(a, 1), right_two(both, 0), 1, 0),
                contract(left_two(below, 1), right_two(right, 0), 1, 0),
            ],
            1,
        )

    def own(first):
        return jnp.concatenate(
            [own_ref[z].reshape(rows, TILE) for z in range(first, first + HALF)], 1
        )

    inv0, inv1 = inverse(w0_ref), inverse(w1_ref)
    x = split(x_ref[...])
    s0 = times_transpose(own(0), inv0)
    s_ref[:, :PANEL] = s0
    rest = own(HALF) - contract(left_two(split(s0), 1), right_two(x, 0), 1, 0)
    s1 = times_transpose(rest, inv1)
    s_ref[:, PANEL:] = s1
    t1 = times(s1, inv1)
    t0 = times(s0 - contract(left_two(split(t1), 1), right_two(x, 1), 1, 1), inv0)
    for start, t in ((0, t0), (PANEL, t1)):
        high = t.astype(jnp.bfloat16)
        t_ref[0, :, start : start + PANEL] = high
        t_ref[1, :, start : start + PANEL] = (t - high.astype(jnp.float32)).astype(jnp.bfloat16)
    c_ref[...] = s_ref[:, tile(col)].reshape(c_ref.shape)

    @pl.when(row < TILES)
    def _():
        c_ref[0] = jnp.zeros((TILE, TILE), jnp.float32)

    for first, w_ref in ((0, w0_ref), (HALF, w1_ref)):

        @pl.when((row >= first) & (row < first + HALF) & (col >= first) & (col <= row))
        def _(first=first, w_ref=w_ref):
            i, j = jnp.clip(col - first, 0, HALF - 1), jnp.clip(row - first, 0, HALF - 1)
            c_ref[0] = w_ref[tile(jnp.where(col == row, HALF + 1, i)), tile(j)].T

    @pl.when((row >= HALF) & (row < TILES) & (col < HALF))
    def _():
        i, j = jnp.clip(col, 0, HALF - 1), jnp.clip(row - HALF, 0, HALF - 1)
        c_ref[0] = x_ref[tile(i), tile(j)].T


def second_kernel(
    ids_ref, w0_ref, near_ref, far_ref, own_hbm, t_hbm, c_hbm,
    t_ref, c_ref, own_ref, sems, x_ref, w1_ref, s_ref, b_ref, *scratch
):
    copy = pltpu.make_async_copy(own_hbm, own_ref, sems.at[0])
    copy.start()
    factor_second(ids_ref, w0_ref, near_ref, far_ref, x_ref, w1_ref, b_ref, *scratch)
    copy.wait()
    apply_inverse(ids_ref, own_ref, w0_ref, x_ref, w1_ref, t_ref, c_ref, s_ref)
    out = [
        pltpu.make_async_copy(t_ref, t_hbm, sems.at[1]),
        pltpu.make_async_copy(c_ref, c_hbm, sems.at[2]),
    ]
    for copy in out:
        copy.start()
    for copy in out:
        copy.wait()


def second(ids, w0, near, far, own):
    rows = own.shape[1] * TILE
    return pl.pallas_call(
        second_kernel,
        out_shape=[
            jax.ShapeDtypeStruct((2, rows, WIDTH), jnp.bfloat16),
            jax.ShapeDtypeStruct((own.shape[1], TILE, TILE), jnp.float32),
        ],
        in_specs=[SMEM, VMEM, VMEM, VMEM, pl.BlockSpec(memory_space=pl.ANY)],
        out_specs=[pl.BlockSpec(memory_space=pltpu.HBM)] * 2,
        scratch_shapes=[
            pltpu.VMEM((2, rows, WIDTH), jnp.bfloat16),
            pltpu.VMEM((own.shape[1], TILE, TILE), jnp.float32),
            pltpu.VMEM(own.shape, jnp.float32),
            pltpu.SemaphoreType.DMA((3,)),
            pltpu.VMEM((PANEL, PANEL), jnp.float32),
            pltpu.VMEM(FACTOR, jnp.float32),
            pltpu.VMEM((rows, WIDTH), jnp.float32),
            pltpu.VMEM((WIDTH, PANEL), jnp.float32),
        ]
        + panel_scratch(),
        compiler_params=pltpu.CompilerParams(vmem_limit_bytes=GRANT),
        cost_estimate=pl.CostEstimate(flops=16 << 30, bytes_accessed=8 << 20, transcendentals=0),
        name="second",
    )(ids, w0, near, far, own)


def update_kernel(ids_ref, t_ref, c_ref, *refs):
    *right_refs, k_ref, o_ref = refs
    n = len(right_refs)
    right = jnp.concatenate(
        [
            jnp.concatenate([ref[x, r, 0] for r in range(TILES) for x in range(4)], 0)
            for ref in right_refs
        ],
        1,
    )
    high = right.astype(jnp.bfloat16)
    low = (right - high.astype(jnp.float32)).astype(jnp.bfloat16)
    left = jnp.concatenate([t_ref[0], t_ref[0], t_ref[1]], 1)
    product = contract(left, jnp.concatenate([high, low, high], 0), 1, 0)
    product = product.reshape(-1, TILE, n * TILE)
    for i in range(n):
        o_ref[:, i] = k_ref[:, i] - product[:, :, i * TILE : (i + 1) * TILE]

    @pl.when(ids_ref[0] < TILES)
    def _():
        o_ref[0] = jnp.zeros(o_ref.shape[1:], jnp.float32)

    @pl.when(pl.program_id(0) == 0)
    def _():
        o_ref[:, 0] = c_ref[...]


def update(ids, t, c, right, kernel):
    tiles, columns = kernel.shape[:2]
    n = 6
    block = pl.BlockSpec((tiles, n, TILE, TILE), lambda j: (0, j, 0, 0))

    def piece(i):
        return pl.BlockSpec(
            (4, TILES, 1, TILE // 4, TILE),
            lambda j: (0, 0, jnp.maximum(n * j + i - 1, 0), 0, 0),
        )

    return pl.pallas_call(
        update_kernel,
        grid=(columns // n,),
        out_shape=jax.ShapeDtypeStruct(kernel.shape, jnp.float32),
        in_specs=[SMEM, VMEM, VMEM] + [piece(i) for i in range(n)] + [block],
        out_specs=block,
        compiler_params=pltpu.CompilerParams(vmem_limit_bytes=60 << 20),
        name="update",
    )(ids, t, c, *[right] * n, kernel)


def swap(x):
    return lax.ppermute(x, "k", [(0, 1), (1, 0)])


def send(x, axis, pairs):
    return lax.ppermute(x, axis, pairs)


def around(block, axis):
    n = lax.axis_size(axis)
    return [block] + [send(block, axis, [(i, (i + d) % n) for i in range(n)]) for d in range(1, n)]


def gather_z(block):
    n = lax.axis_size("z")
    k, z = lax.axis_index("k"), lax.axis_index("z")
    pair = jnp.stack([block, swap(block)])
    parts = []
    for d in (1, 2, 3):
        up = [(i, (i + d) % n) for i in range(n)]
        down = [(n + i, n + (i - d) % n) for i in range(n)]
        parts.append(send(pair, ("k", "z"), up + down))
    far = send(block, "z", [(i, (i + n // 2) % n) for i in range(n)])
    parts, far = lax.optimization_barrier((parts, far))
    mine = jnp.stack([p[0] for p in parts])
    other = swap(jnp.stack([p[1] for p in parts]))
    below = jnp.where(k == 0, mine, other)
    above = jnp.where(k == 0, other, mine)
    ring = jnp.concatenate([block[None], above, far[None], below[::-1]])
    return lax.dynamic_slice_in_dim(jnp.concatenate([ring, ring]), (n - z) % n, n, 0)


def body(kernel):
    kernel = kernel.transpose(0, 2, 1, 3)
    x = lax.axis_index("x")
    y = lax.axis_index("y")
    places = (ROW, "z", "y", "k", "x")
    ids = jnp.stack([lax.axis_index(a) for a in places]).astype(jnp.int32)
    mine, kernel = lax.optimization_barrier((kernel[:, 0], kernel))
    own = lax.all_gather(mine, "z")

    quarters = kernel[0].reshape(-1, 4, TILE // 4, TILE)
    quarter = quarters[:, 0]
    for d in (1, 3, 2):
        quarter = jnp.where(x == d, send(quarters[:, d], "x", [(0, d)]), quarter)
    right = lax.all_gather(quarter[1:], ROW)
    right = right.reshape(4, TILES, -1, TILE // 4, TILE)

    strips = jnp.stack(around(gather_z(quarter[0]), "y"))
    top = [lax.dynamic_index_in_dim(strips, (y + 4 - i) % 4, 0, False)[:HALF] for i in range(2)]
    near = jnp.stack(around(jnp.stack(top), "x"))
    near, rest, own = lax.optimization_barrier((near, strips[:, HALF:], own))
    far = swap(near)
    parts = around(rest, "x")
    w0 = first(ids, near, far)
    w0, parts = lax.optimization_barrier((w0, parts))
    more = jnp.stack(parts)
    t, c = second(ids, w0, more, swap(more), own)
    out = update(ids, t, c, right, kernel)
    return out.transpose(0, 2, 1, 3)


def solution(mesh):
    fine = Mesh(mesh.devices.reshape(4, 4, 2, 8), ("x", "y", "k", "z"))
    spec = P(None, ROW, None, "z")
    return jax.shard_map(body, mesh=fine, in_specs=(spec,), out_specs=spec, check_vma=False)
```
